32 devices in a mesh: section: 4 (over x, core), row: 8 (over z, y).
Axes of the slice: x: 2, y: 2, z: 4, core: 2. Of those that a mesh axis runs over, the one named last changes fastest.
Arguments:
- layer_input: bfloat16 [4, 1024, 4096], P('section', 'row'), may hold values from -6 to 6
- cotangent: bfloat16 [4, 1024, 4096], P('section', 'row'), may hold values from -6 to 6
- route_weight: float32 [4, 1024, 2], P('section', 'row'), may hold values from 0.1 to 0.9
- chosen: int32 [4, 1024, 2], P('section', 'row'), may hold values from 0 to 7, all different within a row
- hot_expert: int32 [4], P('section'), may hold values from 0 to 7
- store_in: bfloat16 [4, 2, 4096, 7168], P('section', None, None, 'row'), may hold values from -0.09375 to 0.09375
- store_out: bfloat16 [4, 7168, 4096], P('section', 'row'), may hold values from -0.0625 to 0.0625
Outputs:
- back_cot: bfloat16 [4, 1024, 4096], P('section', 'row')
- route_grad: float32 [4, 1024, 2], P('section', 'row')
The draws below stay inside these ranges and needn't reach their ends.
Inputs may be any that keep to these rules, and one draw needn't show every extreme that they name: `chosen`: each token names 2 different experts.
All inputs are finite; a program needn't handle non-finite values.
Results may differ from the reference program's by a relative error of at most 0.0034.
Values may be sent and summed in bfloat16 or wider, within the bound.
A program may use at most 64 MiB of HBM per device.

```python
import jax
import jax.numpy as jnp
from jax import lax

D = 4096
FF = 7168
EXPERTS = 8
TOP = 2
TOK_DEV = 128
CAP = 2
SECTIONS = 4
TOKENS = 1024
N_ROW = 8


def plant(entries, stream_key, least, largest):
    place = [jax.random.randint(jax.random.fold_in(stream_key, axis), (), 0, length) for axis, length in enumerate(entries.shape)]
    widest = entries.shape.index(max(entries.shape))
    beside = place[:widest] + [(place[widest] + 1) % entries.shape[widest]] + place[widest + 1:]
    return entries.at[tuple(place)].set(least).at[tuple(beside)].set(largest)


def block_levels(rng, shape, pieces, smallest, high):
    factor_of = 1.0
    for axis_at, blocks in pieces:
        heights = jax.random.uniform(jax.random.fold_in(jax.random.fold_in(rng, 6), axis_at), (blocks,), jnp.float32, smallest / len(pieces), high / len(pieces))
        factor_of = factor_of * jnp.repeat(jnp.exp(heights), shape[axis_at] // blocks).reshape((-1,) + (1,) * (len(shape) - 1 - axis_at))
    return factor_of


def picks_of(key, rows, amount, top, lift):
    ranking = jax.random.permutation(jax.random.fold_in(key, 1), amount)
    favour = ranking
    for power in range(3):
        favour = favour * favour // amount
    favour = favour * lift // amount
    lots = jax.random.randint(jax.random.fold_in(key, 2), (rows, amount), 0, 4096) + favour
    fixed_rows = jax.random.permutation(jax.random.fold_in(key, 3), rows)[jnp.arange(amount) % rows]
    lots = jnp.where(jnp.arange(rows)[:, None] == fixed_rows[None, :], 1 << 14, lots)
    score = lots * amount + jnp.arange(amount)
    return lax.top_k(score.astype(jnp.int32), top)[1].astype(jnp.int32)


def scatter_about(key, dims, deviation, reach, pieces=(), kind=jnp.bfloat16):
    result = deviation * jax.random.normal(key, dims, jnp.float32)
    if pieces:
        result = result * block_levels(key, dims, pieces, -0.22, 0.18)
    return jnp.clip(result, -reach, reach).astype(kind)


def setup_inputs(seed: int = 0) -> dict:
    streams_of = jax.random.split(jax.random.key(seed), 8)
    layer_input = scatter_about(streams_of[0], (SECTIONS, TOKENS, D), 1.0, 6.0, ((0, 4), (1, 8)))
    cotangent = scatter_about(streams_of[1], (SECTIONS, TOKENS, D), 1.0, 6.0, ((0, 4), (1, 8)))
    route_weight = jnp.clip(0.1 + 0.79999997 * jax.random.uniform(streams_of[2], (SECTIONS, TOKENS, TOP), jnp.float32) ** block_levels(streams_of[2], (SECTIONS, TOKENS, TOP), ((0, 4), (1, 8)), -0.2, 0.2), 0.1, 0.9)
    chosen = picks_of(streams_of[3], SECTIONS * TOKENS, EXPERTS, TOP, 4096).reshape((SECTIONS, TOKENS, TOP))
    hot_expert = plant(jax.random.randint(streams_of[4], (SECTIONS,), 0, EXPERTS), jax.random.fold_in(streams_of[4], 1), 0, EXPERTS - 1).astype(jnp.int32)
    store_in = scatter_about(streams_of[5], (SECTIONS, 2, D, FF), D ** -0.5, 0.09375, ((0, 4), (3, 8)))
    store_out = scatter_about(streams_of[6], (SECTIONS, FF, D), FF ** -0.5, 0.0625, ((0, 4), (1, 8)))
    return dict(layer_input=layer_input, cotangent=cotangent, route_weight=route_weight, chosen=chosen, hot_expert=hot_expert, store_in=store_in, store_out=store_out)


def token_select(block_c, hot):
    hit = (block_c == hot).astype(jnp.int32).reshape(-1)
    order = (jnp.cumsum(hit) - hit).astype(jnp.int32)
    held = (hit * (order < CAP).astype(jnp.int32)).astype(jnp.int32)
    slots = (order[None, :] == jnp.arange(CAP, dtype=jnp.int32)[:, None]).astype(jnp.int32) * held[None, :]
    tsel = jnp.sum(slots.reshape(CAP, TOK_DEV, TOP), axis=2).astype(jnp.int32)
    return tsel, held.reshape(TOK_DEV, TOP)


def reference(layer_input, cotangent, route_weight, chosen, hot_expert, store_in, store_out):
    high = lax.Precision.HIGHEST
    moved_all = []
    grad_all = []
    for section in range(SECTIONS):
        hot = hot_expert[section]
        blocks_x = layer_input[section].reshape(N_ROW, TOK_DEV, D)
        blocks_g = cotangent[section].reshape(N_ROW, TOK_DEV, D)
        blocks_w = route_weight[section].reshape(N_ROW, TOK_DEV, TOP)
        blocks_c = chosen[section].reshape(N_ROW, TOK_DEV, TOP)

        def build(items):
            tsel, held = token_select(items[2], hot)
            pick = tsel.astype(jnp.float32)
            rx = jnp.dot(pick, items[0].astype(jnp.float32), precision=high).astype(jnp.bfloat16)
            rg = jnp.dot(pick, items[1].astype(jnp.float32), precision=high).astype(jnp.bfloat16)
            return rx, rg

        rows_x, rows_g = lax.map(build, (blocks_x, blocks_g, blocks_c))
        rows_x = rows_x.reshape(N_ROW * CAP, D).astype(jnp.float32)
        rows_g = rows_g.reshape(N_ROW * CAP, D).astype(jnp.float32)
        w_gate = store_in[section, 0].astype(jnp.float32)
        w_up = store_in[section, 1].astype(jnp.float32)
        w_out = store_out[section].astype(jnp.float32)
        gate = jnp.dot(rows_x, w_gate, precision=high)
        upper = jnp.dot(rows_x, w_up, precision=high)
        sig = jax.nn.sigmoid(gate)
        hidden = (gate * sig * upper).astype(jnp.bfloat16)
        out = jnp.dot(hidden.astype(jnp.float32), w_out, precision=high)
        d_hidden = jnp.dot(rows_g, w_out.T, precision=high)
        d_gate = (d_hidden * upper * sig * (1.0 + gate * (1.0 - sig))).astype(jnp.bfloat16)
        d_up = (d_hidden * gate * sig).astype(jnp.bfloat16)
        back = (jnp.dot(d_gate.astype(jnp.float32), w_gate.T, precision=high) + jnp.dot(d_up.astype(jnp.float32), w_up.T, precision=high)).astype(jnp.bfloat16)
        out_blocks = out.reshape(N_ROW, CAP, D)
        back_blocks = back.reshape(N_ROW, CAP, D)

        def finish(items):
            block_g, block_w, block_c, out_b, back_b = items
            tsel, held = token_select(block_c, hot)
            pick = tsel.astype(jnp.float32)
            out_tok = jnp.dot(pick.T, out_b, precision=high)
            back_tok = jnp.dot(pick.T, back_b.astype(jnp.float32), precision=high)
            weight_tok = jnp.sum(held.astype(jnp.float32) * block_w, axis=1)
            cot = block_g.astype(jnp.float32)
            moved = (cot + weight_tok[:, None] * back_tok).astype(jnp.bfloat16)
            grad = held.astype(jnp.float32) * jnp.sum(cot * out_tok, axis=1)[:, None]
            return moved, grad

        moved, grad = lax.map(finish, (blocks_g, blocks_w, blocks_c, out_blocks, back_blocks))
        moved_all.append(moved.reshape(TOKENS, D))
        grad_all.append(grad.reshape(TOKENS, TOP))
    zeros = jnp.zeros((TOKENS, D), jnp.bfloat16)
    back_cot = jnp.stack(moved_all[1:] + [zeros], axis=0)
    return back_cot, jnp.stack(grad_all, axis=0)
```

```python
import functools

import jax
import jax.numpy as jnp
from jax import lax
from jax.experimental import pallas as pl
from jax.experimental.pallas import tpu as pltpu
from jax.sharding import PartitionSpec as P

CAP = 2
MESH = pl.DeviceIdType.MESH
F32 = jnp.float32
BF16 = jnp.bfloat16
ROWS = 16
PARTS = ROWS // (2 * CAP)
BANDS = ROWS // CAP
HALVES = 2
LAST = (((1,), (1,)), ((), ()))


def iota(shape, dim):
    return lax.broadcasted_iota(jnp.int32, shape, dim)


def expert_kernel(
    n_row, n_sec, hot_ref, chosen_ref, weight_ref, x_hbm, cot_hbm, win_hbm, wout_hbm,
    shift_out, rows_out, scale_out, grad_out,
    x_v, cot_v, win_v, wout_v, gath, xs, gs, zgate, zup, zdh, dgate, dup, back, pack, land,
    scale_v, scale_land, score_v, score_land, zero_v,
    w_sem, t_sem, gath_send, gath_recv, back_send, back_recv, score_send, score_recv,
    small_send, small_recv, shift_send, shift_recv, zero_sem,
):
    sec = lax.axis_index("section")
    me = lax.axis_index("row")
    tokens, width = x_v.shape
    ff = win_v.shape[2]
    slots = n_row * CAP
    part = width // PARTS
    band = width // (HALVES * BANDS)

    def w_copy(i, c):
        if i < 2:
            return pltpu.make_async_copy(
                win_hbm.at[i, pl.ds(c * part, part)], win_v.at[i, pl.ds(c * part, part)], w_sem.at[i, c]
            )
        return pltpu.make_async_copy(
            wout_hbm.at[:, pl.ds(pl.multiple_of(c * part, part), part)], wout_v.at[c], w_sem.at[i, c]
        )

    x_copy = pltpu.make_async_copy(x_hbm, x_v, t_sem.at[0])
    cot_copy = pltpu.make_async_copy(cot_hbm, cot_v, t_sem.at[1])
    x_copy.start()
    cot_copy.start()
    for c in range(PARTS):
        for i in range(3):
            w_copy(i, c).start()

    has_prev = sec > 0
    has_next = sec < n_sec - 1
    barrier = pltpu.get_barrier_semaphore()

    @pl.loop(1, n_row)
    def _(i):
        pl.semaphore_signal(
            barrier, inc=1, device_id={"section": sec, "row": lax.rem(me + i, n_row)}, device_id_type=MESH
        )

    @pl.when(has_prev)
    def _():
        @pl.loop(0, n_row)
        def _(r):
            pl.semaphore_signal(barrier, inc=1, device_id={"section": sec - 1, "row": r}, device_id_type=MESH)

    @pl.when(has_next)
    def _():
        @pl.loop(0, n_row)
        def _(r):
            pl.semaphore_signal(barrier, inc=1, device_id={"section": sec + 1, "row": r}, device_id_type=MESH)

    hit = (chosen_ref[...] == hot_ref[0]).astype(F32)
    hit_tok = jnp.sum(hit, axis=0, keepdims=True)
    before = (iota((tokens, tokens), 0) < iota((tokens, tokens), 1)).astype(BF16)
    order = jnp.dot(
        jnp.broadcast_to(hit_tok, (ROWS, tokens)).astype(BF16), before, preferred_element_type=F32
    )[0:1]
    picks = [jnp.where(order == float(j), hit_tok, 0.0) for j in range(CAP)]
    held = hit * sum(picks)
    weight_tok = jnp.sum(held * weight_ref[...], axis=0, keepdims=True)
    row8 = iota((8, tokens), 0)
    scale = jnp.zeros((8, tokens), F32)
    for j in range(CAP):
        scale = scale + jnp.where(row8 == j, weight_tok * picks[j], 0.0)
    scale_v[...] = scale

    sides = has_prev.astype(jnp.int32) + has_next.astype(jnp.int32)
    pl.semaphore_wait(barrier, n_row - 1 + n_row * sides)

    prev = {"section": sec - 1, "row": me}
    shift = pltpu.make_async_remote_copy(
        cot_hbm, shift_out, shift_send, shift_recv, device_id=prev, device_id_type=MESH
    )
    small = pltpu.make_async_remote_copy(
        scale_v, scale_land, small_send, small_recv, device_id=prev, device_id_type=MESH
    )
    blank = pltpu.make_async_copy(zero_v, shift_out, zero_sem)

    x_copy.wait()
    cot_copy.wait()
    lead = iota((ROWS, tokens), 0)
    block = jnp.zeros((ROWS, part), F32)
    for c in range(PARTS):
        for side, source in enumerate((x_v, cot_v)):
            one = jnp.zeros((ROWS, tokens), F32)
            for j in range(CAP):
                one = one + jnp.where(lead == c * 2 * CAP + side * CAP + j, picks[j], 0.0)
            block = block + jnp.dot(
                one.astype(BF16), source[:, c * part : (c + 1) * part], preferred_element_type=F32
            )
    gath[pl.ds(me, 1)] = block.astype(BF16)[None]

    def gath_copy(i):
        to = lax.rem(me + i, n_row)
        return pltpu.make_async_remote_copy(
            gath.at[me], gath.at[me], gath_send.at[to], gath_recv.at[me],
            device_id={"section": sec, "row": to}, device_id_type=MESH,
        )

    def gath_wait(i):
        src = lax.rem(me + i, n_row)
        return pltpu.make_async_remote_copy(
            gath.at[src], gath.at[src], gath_send.at[src], gath_recv.at[src],
            device_id={"section": sec, "row": src}, device_id_type=MESH,
        )

    @pl.loop(1, n_row)
    def _(i):
        gath_copy(i).start()

    @pl.when(has_prev)
    def _():
        shift.start()
        small.start()

    @pl.when(jnp.logical_not(has_next))
    def _():
        zero_v[...] = jnp.zeros_like(zero_v)
        blank.start()

    @pl.loop(1, n_row)
    def _(i):
        gath_wait(i).wait_recv()

    everyone = gath[...].reshape(n_row * ROWS, part)
    to_row = iota((2 * slots, n_row * ROWS), 0)
    from_row = iota((2 * slots, n_row * ROWS), 1)
    slot = lax.rem(to_row, slots)
    want = (slot // CAP) * ROWS + (to_row // slots) * CAP + lax.rem(slot, CAP)
    for c in range(PARTS):
        sel = (from_row == want + c * 2 * CAP).astype(BF16)
        both = jnp.dot(sel, everyone, preferred_element_type=F32).astype(BF16)
        xs[c] = both[:slots]
        gs[c] = both[slots:]

    zgate[...] = jnp.zeros_like(zgate)
    zup[...] = jnp.zeros_like(zup)
    zdh[...] = jnp.zeros_like(zdh)

    @pl.loop(0, PARTS)
    def _(c):
        rows = pl.ds(pl.multiple_of(c * part, part), part)
        w_copy(0, c).wait()
        zgate[...] += jnp.dot(xs[c], win_v[0, rows, :], preferred_element_type=F32)
        w_copy(1, c).wait()
        zup[...] += jnp.dot(xs[c], win_v[1, rows, :], preferred_element_type=F32)
        w_copy(2, c).wait()
        zdh[...] += lax.dot_general(wout_v[c], gs[c], LAST, preferred_element_type=F32)

    gate, up, dh = zgate[...], zup[...], zdh[...].T
    sig = jax.nn.sigmoid(gate)
    hidden = (gate * sig * up).astype(BF16)
    dgate[...] = (dh * up * sig * (1.0 + gate * (1.0 - sig))).astype(BF16)
    dup[...] = (dh * gate * sig).astype(BF16)
    score = jnp.sum(hidden.astype(F32) * dh, axis=1, keepdims=True)
    diag = iota((slots, 128), 0) == iota((slots, 128), 1)
    score_row = jnp.sum(jnp.where(diag, score, 0.0), axis=0, keepdims=True)
    score_v[...] = jnp.broadcast_to(score_row, score_v.shape)

    def score_copy(to, slot_of):
        return pltpu.make_async_remote_copy(
            score_v, score_land.at[slot_of], score_send.at[to], score_recv.at[slot_of],
            device_id={"section": sec, "row": to}, device_id_type=MESH,
        )

    @pl.loop(1, n_row)
    def _(i):
        score_copy(lax.rem(me + i, n_row), me).start()

    score_land[pl.ds(me, 1)] = score_v[...][None]

    def back_copy(h, r, slot_of):
        return pltpu.make_async_remote_copy(
            pack.at[h, r], land.at[h, slot_of], back_send.at[h, r], back_recv.at[h, slot_of],
            device_id={"section": sec - 1, "row": r}, device_id_type=MESH,
        )

    @pl.when(has_prev)
    def _():
        per = PARTS // HALVES

        @pl.loop(0, HALVES)
        def _(h):
            for q in range(per):
                rows = pl.ds(pl.multiple_of((h * per + q) * part, part), part)
                total = lax.dot_general(win_v[0, rows, :], dgate[...], LAST, preferred_element_type=F32)
                total = total + lax.dot_general(win_v[1, rows, :], dup[...], LAST, preferred_element_type=F32)
                back[:, q * part : (q + 1) * part] = total.T.astype(BF16)
            stack = jnp.concatenate([back[:, b * band : (b + 1) * band] for b in range(BANDS)], axis=0)
            out_row = iota((n_row * ROWS, BANDS * slots), 0)
            in_row = iota((n_row * ROWS, BANDS * slots), 1)
            inner = lax.rem(out_row, ROWS)
            source = (inner // CAP) * slots + (out_row // ROWS) * CAP + lax.rem(inner, CAP)
            perm = (in_row == source).astype(BF16)
            packed = jnp.dot(perm, stack, preferred_element_type=F32).astype(BF16)
            pack[pl.ds(h, 1)] = packed.reshape(1, n_row, ROWS, band)

            @pl.loop(0, n_row)
            def _(r):
                back_copy(h, r, me).start()

    @pl.loop(1, n_row)
    def _(i):
        score_copy(lax.rem(me + i, n_row), lax.rem(me + i, n_row)).wait_recv()

    sums = jnp.sum(score_land[...], axis=0)
    lane = iota(sums.shape, 1)
    grad_tok = jnp.zeros((1, tokens), F32)
    for j in range(CAP):
        mine = jnp.sum(jnp.where(lane == me * CAP + j, sums, 0.0), axis=1, keepdims=True)[0:1]
        grad_tok = grad_tok + picks[j] * mine
    grad_out[...] = held * grad_tok

    @pl.when(has_next)
    def _():
        @pl.loop(0, HALVES)
        def _(h):
            @pl.loop(0, n_row)
            def _(r):
                back_copy(h, r, r).wait_recv()

            total = jnp.sum(land[pl.ds(h, 1)][0].astype(F32), axis=0)
            rows_out[pl.ds(h, 1)] = total.astype(BF16).astype(F32)[None]

        small.wait_recv()
        shift.wait_recv()
        scale_out[...] = scale_land[...]

    @pl.when(jnp.logical_not(has_next))
    def _():
        rows_out[...] = jnp.zeros_like(rows_out)
        scale_out[...] = jnp.zeros_like(scale_out)
        blank.wait()

    @pl.loop(1, n_row)
    def _(i):
        gath_copy(i).wait_send()
        score_copy(lax.rem(me + i, n_row), me).wait_send()

    @pl.when(has_prev)
    def _():
        shift.wait_send()
        small.wait_send()

        @pl.loop(0, HALVES)
        def _(h):
            @pl.loop(0, n_row)
            def _(r):
                back_copy(h, r, me).wait_send()


def merge_kernel(shift_ref, rows_ref, scale_ref, out_ref):
    tokens = shift_ref.shape[0]
    band = rows_ref.shape[2]
    diag = iota((tokens, tokens), 0) == iota((tokens, tokens), 1)
    cols = [
        jnp.sum(jnp.where(diag, scale_ref[j : j + 1, :], 0.0), axis=1, keepdims=True) for j in range(CAP)
    ]
    for b in range(BANDS):
        at = slice(b * band, (b + 1) * band)
        value = shift_ref[:, at].astype(F32)
        for j in range(CAP):
            value = value + cols[j] * rows_ref[0, b * CAP + j : b * CAP + j + 1, :]
        out_ref[:, at] = value.astype(BF16)


def on_device(n_row, n_sec, layer_input, cotangent, route_weight, chosen, hot_expert, store_in, store_out):
    _, tokens, width = layer_input.shape
    ff = store_out.shape[1]
    top = chosen.shape[2]
    slots = n_row * CAP
    part = width // PARTS
    band = width // (HALVES * BANDS)
    hbm = pl.BlockSpec(memory_space=pl.ANY)
    vmem = pl.BlockSpec(memory_space=pltpu.VMEM)
    dma = pltpu.SemaphoreType.DMA
    shift, rows, scale, grad = pl.pallas_call(
        functools.partial(expert_kernel, n_row, n_sec),
        out_shape=(
            jax.ShapeDtypeStruct((tokens, width), BF16),
            jax.ShapeDtypeStruct((HALVES, ROWS, band), F32),
            jax.ShapeDtypeStruct((8, tokens), F32),
            jax.ShapeDtypeStruct((top, tokens), F32),
        ),
        in_specs=[pl.BlockSpec(memory_space=pltpu.SMEM), vmem, vmem, hbm, hbm, hbm, hbm],
        out_specs=(hbm, vmem, vmem, vmem),
        scratch_shapes=[
            pltpu.VMEM((tokens, width), BF16),
            pltpu.VMEM((tokens, width), BF16),
            pltpu.VMEM((2, width, ff), BF16),
            pltpu.VMEM((PARTS, ff, part), BF16),
            pltpu.VMEM((n_row, ROWS, part), BF16),
            pltpu.VMEM((PARTS, slots, part), BF16),
            pltpu.VMEM((PARTS, slots, part), BF16),
            pltpu.VMEM((slots, ff), F32),
            pltpu.VMEM((slots, ff), F32),
            pltpu.VMEM((ff, slots), F32),
            pltpu.VMEM((slots, ff), BF16),
            pltpu.VMEM((slots, ff), BF16),
            pltpu.VMEM((slots, width // HALVES), BF16),
            pltpu.VMEM((HALVES, n_row, ROWS, band), BF16),
            pltpu.VMEM((HALVES, n_row, ROWS, band), BF16),
            pltpu.VMEM((8, tokens), F32),
            pltpu.VMEM((8, tokens), F32),
            pltpu.VMEM((8, 128), F32),
            pltpu.VMEM((n_row, 8, 128), F32),
            pltpu.VMEM((tokens, width), BF16),
            dma((3, PARTS)),
            dma((2,)),
            dma((n_row,)),
            dma((n_row,)),
            dma((HALVES, n_row)),
            dma((HALVES, n_row)),
            dma((n_row,)),
            dma((n_row,)),
            dma,
            dma,
            dma,
            dma,
            dma,
        ],
        compiler_params=pltpu.CompilerParams(
            collective_id=0, has_side_effects=True, vmem_limit_bytes=60 * 2**20
        ),
        cost_estimate=pl.CostEstimate(
            flops=10 * slots * width * ff, bytes_accessed=6 * width * ff, transcendentals=slots * ff
        ),
        name="expert",
    )(
        hot_expert,
        jnp.transpose(chosen[0]),
        jnp.transpose(route_weight[0]),
        layer_input[0],
        cotangent[0],
        store_in[0],
        store_out[0],
    )
    half = width // HALVES
    moved = pl.pallas_call(
        merge_kernel,
        out_shape=jax.ShapeDtypeStruct((tokens, width), BF16),
        grid=(HALVES,),
        in_specs=[
            pl.BlockSpec((tokens, half), lambda h: (0, h)),
            pl.BlockSpec((1, ROWS, band), lambda h: (h, 0, 0)),
            pl.BlockSpec((8, tokens), lambda h: (0, 0)),
        ],
        out_specs=pl.BlockSpec((tokens, half), lambda h: (0, h)),
        name="merge",
    )(shift, rows, scale)
    return (moved[None], jnp.transpose(grad)[None])


def token_select(block_c, hot, slot_count):
    count_tok, top_count = block_c.shape
    hit = (block_c == hot).astype(jnp.int32).reshape(-1)
    order = jnp.cumsum(hit) - hit
    held = hit * (order < slot_count).astype(jnp.int32)
    slots = (order[None, :] == jnp.arange(slot_count, dtype=jnp.int32)[:, None]).astype(
        jnp.int32
    ) * held[None, :]
    tsel = jnp.sum(slots.reshape(slot_count, count_tok, top_count), axis=2)
    return (tsel, held.reshape(count_tok, top_count))


def on_device_narrow(layer_input, cotangent, route_weight, chosen, hot_expert, store_in, store_out):
    tokens_here = layer_input[0]
    cot_here = cotangent[0]
    width = tokens_here.shape[1]
    num_row = lax.axis_size("row")
    size = lax.axis_size("section")
    tsel, held = token_select(chosen[0], hot_expert[0], CAP)
    pick = tsel.astype(BF16)
    rows = jnp.concatenate(
        [jnp.dot(pick, part, preferred_element_type=F32).astype(BF16) for part in (tokens_here, cot_here)], axis=1
    )
    both = lax.all_gather(rows, "row", axis=0, tiled=True)
    all_x, all_g = both[:, :width], both[:, width:]
    w_gate, w_up, w_out = store_in[0, 0], store_in[0, 1], store_out[0]
    gate = jnp.dot(all_x, w_gate, preferred_element_type=F32)
    upper = jnp.dot(all_x, w_up, preferred_element_type=F32)
    sig = jax.nn.sigmoid(gate)
    hidden = (gate * sig * upper).astype(BF16)
    d_hidden = lax.dot_general(all_g, w_out, LAST, preferred_element_type=F32)
    d_gate = (d_hidden * upper * sig * (1.0 + gate * (1.0 - sig))).astype(BF16)
    d_up = (d_hidden * gate * sig).astype(BF16)
    back_part = lax.dot_general(d_gate, w_gate, LAST, preferred_element_type=F32) + lax.dot_general(
        d_up, w_up, LAST, preferred_element_type=F32
    )
    score_part = jnp.sum(hidden.astype(F32) * d_hidden, axis=1)
    got_back = lax.all_to_all(
        back_part.reshape(num_row, CAP, width), "row", split_axis=0, concat_axis=0, tiled=True
    )
    got_score = lax.all_to_all(
        score_part.reshape(num_row, CAP), "row", split_axis=0, concat_axis=0, tiled=True
    )
    back_rows = jnp.sum(got_back, axis=0).astype(BF16)
    slot_score = jnp.sum(got_score, axis=0)
    back_tok = jnp.dot(pick.T, back_rows, preferred_element_type=F32)
    score_tok = jnp.sum(tsel.astype(F32).T * slot_score[None, :], axis=1)
    weight_tok = jnp.sum(held.astype(F32) * route_weight[0], axis=1)
    moved = (cot_here.astype(F32) + weight_tok[:, None] * back_tok).astype(BF16)
    route_grad = held.astype(F32) * score_tok[:, None]
    back_cot = lax.ppermute(moved, "section", [(i, i - 1) for i in range(1, size)])
    return (back_cot[None], route_grad[None])


def solution(mesh):
    n_row, n_sec = mesh.shape["row"], mesh.shape["section"]

    def body(layer_input, cotangent, route_weight, chosen, hot_expert, store_in, store_out):
        args = (layer_input, cotangent, route_weight, chosen, hot_expert, store_in, store_out)
        if store_out.shape[1] % 128 or n_row * CAP > 128:
            return on_device_narrow(*args)
        return on_device(n_row, n_sec, *args)

    in_specs = (
        P("section", "row", None),
        P("section", "row", None),
        P("section", "row", None),
        P("section", "row", None),
        P("section"),
        P("section", None, None, "row"),
        P("section", "row", None),
    )
    out_specs = (P("section", "row", None), P("section", "row", None))
    return jax.shard_map(body, mesh=mesh, in_specs=in_specs, out_specs=out_specs, check_vma=False)
```

```python
import functools

import jax
import jax.numpy as jnp
from jax import lax
from jax.experimental import pallas as pl
from jax.experimental.pallas import tpu as pltpu
from jax.sharding import PartitionSpec as P

CAP = 2
MESH = pl.DeviceIdType.MESH
F32 = jnp.float32
BF16 = jnp.bfloat16
ROWS = 16
BANDS = ROWS // CAP
QUARTERS = 4
LAST = (((1,), (1,)), ((), ()))


def iota(shape, dim):
    return lax.broadcasted_iota(jnp.int32, shape, dim)


def expert_kernel(
    n_row, n_sec, hot_ref, chosen_ref, weight_ref, x_hbm, cot_hbm, win_hbm, wout_hbm,
    shift_out, rows_out, scale_out, grad_out,
    x_v, cot_v, win_v, wout_v, gath, xs, gs, pack, land,
    scale_v, scale_land, score_v, score_land, zero_v,
    win_sem, wout_sem, t_sem, gath_send, gath_recv, back_send, back_recv, score_send, score_recv,
    small_send, small_recv, shift_send, shift_recv, zero_sem,
):
    sec = lax.axis_index("section")
    me = lax.axis_index("row")
    tokens, width = x_v.shape
    slots = n_row * CAP
    part = width // BANDS
    quarter = width // QUARTERS
    band = quarter // BANDS

    def win_copy(i, c):
        rows = pl.ds(c * quarter, quarter)
        return pltpu.make_async_copy(win_hbm.at[i, rows], win_v.at[i, rows], win_sem.at[i, c])

    wout_copy = pltpu.make_async_copy(wout_hbm, wout_v, wout_sem)
    x_copy = pltpu.make_async_copy(x_hbm, x_v, t_sem.at[0])
    cot_copy = pltpu.make_async_copy(cot_hbm, cot_v, t_sem.at[1])
    x_copy.start()
    cot_copy.start()

    has_prev = sec > 0
    has_next = sec < n_sec - 1
    barrier = pltpu.get_barrier_semaphore()

    @pl.loop(1, n_row)
    def _(i):
        pl.semaphore_signal(
            barrier, inc=1, device_id={"section": sec, "row": lax.rem(me + i, n_row)}, device_id_type=MESH
        )

    @pl.when(has_prev)
    def _():
        @pl.loop(0, n_row)
        def _(r):
            pl.semaphore_signal(barrier, inc=1, device_id={"section": sec - 1, "row": r}, device_id_type=MESH)

    @pl.when(has_next)
    def _():
        @pl.loop(0, n_row)
        def _(r):
            pl.semaphore_signal(barrier, inc=1, device_id={"section": sec + 1, "row": r}, device_id_type=MESH)

    hit = (chosen_ref[...] == hot_ref[0]).astype(F32)
    hit_tok = jnp.sum(hit, axis=0, keepdims=True)
    before = (iota((tokens, tokens), 0) < iota((tokens, tokens), 1)).astype(BF16)
    order = jnp.dot(
        jnp.broadcast_to(hit_tok, (ROWS, tokens)).astype(BF16), before, preferred_element_type=F32
    )[0:1]
    picks = [jnp.where(order == float(j), hit_tok, 0.0) for j in range(CAP)]
    held = hit * sum(picks)
    weight_tok = jnp.sum(held * weight_ref[...], axis=0, keepdims=True)
    row8 = iota((8, tokens), 0)
    scale = jnp.zeros((8, tokens), F32)
    for j in range(CAP):
        scale = scale + jnp.where(row8 == j, weight_tok * picks[j], 0.0)
    scale_v[...] = scale

    lead = iota((ROWS, tokens), 0)
    ones = []
    for c in range(BANDS):
        one = jnp.zeros((ROWS, tokens), F32)
        for j in range(CAP):
            one = one + jnp.where(lead == c * CAP + j, picks[j], 0.0)
        ones.append(one.astype(BF16))

    def held_rows(source):
        block = jnp.zeros((ROWS, part), F32)
        for c in range(BANDS):
            block = block + jnp.dot(
                ones[c], source[:, c * part : (c + 1) * part], preferred_element_type=F32
            )
        return block.astype(BF16)

    def gath_copy(k, to, slot_of):
        return pltpu.make_async_remote_copy(
            gath.at[k, slot_of], gath.at[k, slot_of], gath_send.at[k, to], gath_recv.at[k, slot_of],
            device_id={"section": sec, "row": to}, device_id_type=MESH,
        )

    prev = {"section": sec - 1, "row": me}
    shift = pltpu.make_async_remote_copy(
        cot_hbm, shift_out, shift_send, shift_recv, device_id=prev, device_id_type=MESH
    )
    small = pltpu.make_async_remote_copy(
        scale_v, scale_land, small_send, small_recv, device_id=prev, device_id_type=MESH
    )
    blank = pltpu.make_async_copy(zero_v, shift_out, zero_sem)

    x_copy.wait()
    gath[0, pl.ds(me, 1)] = held_rows(x_v)[None]

    sides = has_prev.astype(jnp.int32) + has_next.astype(jnp.int32)
    pl.semaphore_wait(barrier, n_row - 1 + n_row * sides)

    @pl.loop(1, n_row)
    def _(i):
        gath_copy(0, lax.rem(me + i, n_row), me).start()

    cot_copy.wait()
    for c in range(QUARTERS):
        win_copy(0, c).start()
        win_copy(1, c).start()
    wout_copy.start()

    gath[1, pl.ds(me, 1)] = held_rows(cot_v)[None]

    @pl.loop(1, n_row)
    def _(i):
        gath_copy(1, lax.rem(me + i, n_row), me).start()

    @pl.when(has_prev)
    def _():
        shift.start()
        small.start()

    @pl.when(jnp.logical_not(has_next))
    def _():
        zero_v[...] = jnp.zeros_like(zero_v)
        blank.start()

    to_row = iota((BANDS * slots, n_row * ROWS), 0)
    slot = lax.rem(to_row, slots)
    want = (slot // CAP) * ROWS + (to_row // slots) * CAP + lax.rem(slot, CAP)
    spread = (iota((BANDS * slots, n_row * ROWS), 1) == want).astype(BF16)

    def gathered(k, rows_ref):
        @pl.loop(1, n_row)
        def _(i):
            src = lax.rem(me + i, n_row)
            gath_copy(k, src, src).wait_recv()

        everyone = gath[k].reshape(n_row * ROWS, part)
        rows = jnp.dot(spread, everyone, preferred_element_type=F32).astype(BF16)
        for c in range(BANDS):
            rows_ref[:, c * part : (c + 1) * part] = rows[c * slots : (c + 1) * slots]

    gathered(0, xs)
    gate = up = None
    for c in range(QUARTERS):
        cols = slice(c * quarter, (c + 1) * quarter)
        win_copy(0, c).wait()
        win_copy(1, c).wait()
        g_part = jnp.dot(xs[:, cols], win_v[0, cols, :], preferred_element_type=F32)
        u_part = jnp.dot(xs[:, cols], win_v[1, cols, :], preferred_element_type=F32)
        gate = g_part if gate is None else gate + g_part
        up = u_part if up is None else up + u_part

    gathered(1, gs)
    wout_copy.wait()
    dh = lax.dot_general(wout_v[...], gs[...], LAST, preferred_element_type=F32).T

    sig = jax.nn.sigmoid(gate)
    hidden = (gate * sig * up).astype(BF16)
    dgate = (dh * up * sig * (1.0 + gate * (1.0 - sig))).astype(BF16)
    dup = (dh * gate * sig).astype(BF16)
    score = jnp.sum(hidden.astype(F32) * dh, axis=1, keepdims=True)
    diag = iota((slots, 128), 0) == iota((slots, 128), 1)
    score_row = jnp.sum(jnp.where(diag, score, 0.0), axis=0, keepdims=True)
    score_v[...] = jnp.broadcast_to(score_row, score_v.shape)

    def score_copy(to, slot_of):
        return pltpu.make_async_remote_copy(
            score_v, score_land.at[slot_of], score_send.at[to], score_recv.at[slot_of],
            device_id={"section": sec, "row": to}, device_id_type=MESH,
        )

    @pl.loop(1, n_row)
    def _(i):
        score_copy(lax.rem(me + i, n_row), me).start()

    score_land[pl.ds(me, 1)] = score_v[...][None]

    def back_copy(q, r, slot_of):
        return pltpu.make_async_remote_copy(
            pack.at[q, r], land.at[q, slot_of], back_send.at[q, r], back_recv.at[q, slot_of],
            device_id={"section": sec - 1, "row": r}, device_id_type=MESH,
        )

    @pl.when(has_prev)
    def _():
        out_row = iota((n_row * ROWS, BANDS * slots), 0)
        inner = lax.rem(out_row, ROWS)
        source = (inner // CAP) * slots + (out_row // ROWS) * CAP + lax.rem(inner, CAP)
        perm = (iota((n_row * ROWS, BANDS * slots), 1) == source).astype(BF16)
        for q in range(QUARTERS):
            rows = slice(q * quarter, (q + 1) * quarter)
            total = lax.dot_general(win_v[0, rows, :], dgate, LAST, preferred_element_type=F32)
            total = total + lax.dot_general(win_v[1, rows, :], dup, LAST, preferred_element_type=F32)
            back = total.T.astype(BF16)
            stack = jnp.concatenate([back[:, b * band : (b + 1) * band] for b in range(BANDS)], axis=0)
            packed = jnp.dot(perm, stack, preferred_element_type=F32).astype(BF16)
            pack[q] = packed.reshape(n_row, ROWS, band)

            @pl.loop(0, n_row)
            def _(r):
                back_copy(q, r, me).start()

    @pl.loop(1, n_row)
    def _(i):
        src = lax.rem(me + i, n_row)
        score_copy(src, src).wait_recv()

    sums = jnp.sum(score_land[...], axis=0)
    lane = iota(sums.shape, 1)
    grad_tok = jnp.zeros((1, tokens), F32)
    for j in range(CAP):
        mine = jnp.sum(jnp.where(lane == me * CAP + j, sums, 0.0), axis=1, keepdims=True)[0:1]
        grad_tok = grad_tok + picks[j] * mine
    grad_out[...] = held * grad_tok

    @pl.when(has_next)
    def _():
        small.wait_recv()
        scale_out[...] = scale_land[...]
        shift.wait_recv()
        for q in range(QUARTERS):
            @pl.loop(0, n_row)
            def _(r):
                back_copy(q, r, r).wait_recv()

            rows_out[q] = jnp.sum(land[q].astype(F32), axis=0).astype(BF16).astype(F32)

    @pl.when(jnp.logical_not(has_next))
    def _():
        rows_out[...] = jnp.zeros_like(rows_out)
        scale_out[...] = jnp.zeros_like(scale_out)
        blank.wait()

    @pl.loop(1, n_row)
    def _(i):
        to = lax.rem(me + i, n_row)
        gath_copy(0, to, me).wait_send()
        gath_copy(1, to, me).wait_send()
        score_copy(to, me).wait_send()

    @pl.when(has_prev)
    def _():
        shift.wait_send()
        small.wait_send()

        @pl.loop(0, n_row)
        def _(r):
            for q in range(QUARTERS):
                back_copy(q, r, me).wait_send()


def merge_kernel(shift_ref, rows_ref, scale_ref, grad_ref, out_ref, grad_out, cols):
    tokens = shift_ref.shape[0]
    band = rows_ref.shape[2]

    @pl.when(pl.program_id(0) == 0)
    def _():
        grad_out[...] = grad_ref[...]
        diag = iota((tokens, tokens), 0) == iota((tokens, tokens), 1)
        for j in range(CAP):
            col = jnp.sum(jnp.where(diag, scale_ref[j : j + 1, :], 0.0), axis=1, keepdims=True)
            cols[j] = jnp.broadcast_to(col, (tokens, band))

    for b in range(BANDS):
        at = slice(b * band, (b + 1) * band)
        value = shift_ref[:, at].astype(F32)
        for j in range(CAP):
            value = value + cols[j] * rows_ref[0, b * CAP + j : b * CAP + j + 1, :]
        out_ref[:, at] = value.astype(BF16)


def on_device(n_row, n_sec, layer_input, cotangent, route_weight, chosen, hot_expert, store_in, store_out):
    _, tokens, width = layer_input.shape
    ff = store_out.shape[1]
    top = chosen.shape[2]
    slots = n_row * CAP
    part = width // BANDS
    quarter = width // QUARTERS
    band = quarter // BANDS
    hbm = pl.BlockSpec(memory_space=pl.ANY)
    vmem = pl.BlockSpec(memory_space=pltpu.VMEM)
    dma = pltpu.SemaphoreType.DMA
    shift, rows, scale, grad = pl.pallas_call(
        functools.partial(expert_kernel, n_row, n_sec),
        out_shape=(
            jax.ShapeDtypeStruct((tokens, width), BF16),
            jax.ShapeDtypeStruct((QUARTERS, ROWS, band), F32),
            jax.ShapeDtypeStruct((8, tokens), F32),
            jax.ShapeDtypeStruct((top, tokens), F32),
        ),
        in_specs=[pl.BlockSpec(memory_space=pltpu.SMEM), vmem, vmem, hbm, hbm, hbm, hbm],
        out_specs=(hbm, vmem, vmem, vmem),
        scratch_shapes=[
            pltpu.VMEM((tokens, width), BF16),
            pltpu.VMEM((tokens, width), BF16),
            pltpu.VMEM((2, width, ff), BF16),
            pltpu.VMEM((ff, width), BF16),
            pltpu.VMEM((2, n_row, ROWS, part), BF16),
            pltpu.VMEM((slots, width), BF16),
            pltpu.VMEM((slots, width), BF16),
            pltpu.VMEM((QUARTERS, n_row, ROWS, band), BF16),
            pltpu.VMEM((QUARTERS, n_row, ROWS, band), BF16),
            pltpu.VMEM((8, tokens), F32),
            pltpu.VMEM((8, tokens), F32),
            pltpu.VMEM((8, 128), F32),
            pltpu.VMEM((n_row, 8, 128), F32),
            pltpu.VMEM((tokens, width), BF16),
            dma((2, QUARTERS)),
            dma,
            dma((2,)),
            dma((2, n_row)),
            dma((2, n_row)),
            dma((QUARTERS, n_row)),
            dma((QUARTERS, n_row)),
            dma((n_row,)),
            dma((n_row,)),
            dma,
            dma,
            dma,
            dma,
            dma,
        ],
        compiler_params=pltpu.CompilerParams(
            collective_id=0, has_side_effects=True, vmem_limit_bytes=60 * 2**20
        ),
        cost_estimate=pl.CostEstimate(
            flops=10 * slots * width * ff, bytes_accessed=6 * width * ff, transcendentals=slots * ff
        ),
        name="expert",
    )(
        hot_expert,
        jnp.transpose(chosen[0]),
        jnp.transpose(route_weight[0]),
        layer_input[0],
        cotangent[0],
        store_in[0],
        store_out[0],
    )
    moved, grad = pl.pallas_call(
        merge_kernel,
        out_shape=(
            jax.ShapeDtypeStruct((tokens, width), BF16),
            jax.ShapeDtypeStruct((top, tokens), F32),
        ),
        grid=(QUARTERS,),
        in_specs=[
            pl.BlockSpec((tokens, quarter), lambda q: (0, q)),
            pl.BlockSpec((1, ROWS, band), lambda q: (q, 0, 0)),
            pl.BlockSpec((8, tokens), lambda q: (0, 0)),
            pl.BlockSpec((top, tokens), lambda q: (0, 0)),
        ],
        out_specs=(
            pl.BlockSpec((tokens, quarter), lambda q: (0, q)),
            pl.BlockSpec((top, tokens), lambda q: (0, 0)),
        ),
        scratch_shapes=[pltpu.VMEM((CAP, tokens, band), F32)],
        name="merge",
    )(shift, rows, scale, grad)
    return (moved[None], jnp.transpose(grad)[None])


def token_select(block_c, hot, slot_count):
    count_tok, top_count = block_c.shape
    hit = (block_c == hot).astype(jnp.int32).reshape(-1)
    order = jnp.cumsum(hit) - hit
    held = hit * (order < slot_count).astype(jnp.int32)
    slots = (order[None, :] == jnp.arange(slot_count, dtype=jnp.int32)[:, None]).astype(
        jnp.int32
    ) * held[None, :]
    tsel = jnp.sum(slots.reshape(slot_count, count_tok, top_count), axis=2)
    return (tsel, held.reshape(count_tok, top_count))


def on_device_narrow(layer_input, cotangent, route_weight, chosen, hot_expert, store_in, store_out):
    tokens_here = layer_input[0]
    cot_here = cotangent[0]
    width = tokens_here.shape[1]
    num_row = lax.axis_size("row")
    size = lax.axis_size("section")
    tsel, held = token_select(chosen[0], hot_expert[0], CAP)
    pick = tsel.astype(BF16)
    rows = jnp.concatenate(
        [jnp.dot(pick, part, preferred_element_type=F32).astype(BF16) for part in (tokens_here, cot_here)], axis=1
    )
    both = lax.all_gather(rows, "row", axis=0, tiled=True)
    all_x, all_g = both[:, :width], both[:, width:]
    w_gate, w_up, w_out = store_in[0, 0], store_in[0, 1], store_out[0]
    gate = jnp.dot(all_x, w_gate, preferred_element_type=F32)
    upper = jnp.dot(all_x, w_up, preferred_element_type=F32)
    sig = jax.nn.sigmoid(gate)
    hidden = (gate * sig * upper).astype(BF16)
    d_hidden = lax.dot_general(all_g, w_out, LAST, preferred_element_type=F32)
    d_gate = (d_hidden * upper * sig * (1.0 + gate * (1.0 - sig))).astype(BF16)
    d_up = (d_hidden * gate * sig).astype(BF16)
    back_part = lax.dot_general(d_gate, w_gate, LAST, preferred_element_type=F32) + lax.dot_general(
        d_up, w_up, LAST, preferred_element_type=F32
    )
    score_part = jnp.sum(hidden.astype(F32) * d_hidden, axis=1)
    got_back = lax.all_to_all(
        back_part.reshape(num_row, CAP, width), "row", split_axis=0, concat_axis=0, tiled=True
    )
    got_score = lax.all_to_all(
        score_part.reshape(num_row, CAP), "row", split_axis=0, concat_axis=0, tiled=True
    )
    back_rows = jnp.sum(got_back, axis=0).astype(BF16)
    slot_score = jnp.sum(got_score, axis=0)
    back_tok = jnp.dot(pick.T, back_rows, preferred_element_type=F32)
    score_tok = jnp.sum(tsel.astype(F32).T * slot_score[None, :], axis=1)
    weight_tok = jnp.sum(held.astype(F32) * route_weight[0], axis=1)
    moved = (cot_here.astype(F32) + weight_tok[:, None] * back_tok).astype(BF16)
    route_grad = held.astype(F32) * score_tok[:, None]
    back_cot = lax.ppermute(moved, "section", [(i, i - 1) for i in range(1, size)])
    return (back_cot[None], route_grad[None])


def solution(mesh):
    n_row, n_sec = mesh.shape["row"], mesh.shape["section"]

    def body(layer_input, cotangent, route_weight, chosen, hot_expert, store_in, store_out):
        args = (layer_input, cotangent, route_weight, chosen, hot_expert, store_in, store_out)
        if store_out.shape[1] % 128 or n_row * CAP > 128:
            return on_device_narrow(*args)
        return on_device(n_row, n_sec, *args)

    in_specs = (
        P("section", "row", None),
        P("section", "row", None),
        P("section", "row", None),
        P("section", "row", None),
        P("section"),
        P("section", None, None, "row"),
        P("section", "row", None),
    )
    out_specs = (P("section", "row", None), P("section", "row", None))
    return jax.shard_map(body, mesh=mesh, in_specs=in_specs, out_specs=out_specs, check_vma=False)
```

```python
import functools

import jax
import jax.numpy as jnp
from jax import lax
from jax.experimental import pallas as pl
from jax.experimental.pallas import tpu as pltpu
from jax.sharding import PartitionSpec as P

CAP = 2
MESH = pl.DeviceIdType.MESH
F32 = jnp.float32
BF16 = jnp.bfloat16
ROWS = 16
BANDS = ROWS // CAP
QUARTERS = 4
LAST = (((1,), (1,)), ((), ()))


def iota(shape, dim):
    return lax.broadcasted_iota(jnp.int32, shape, dim)


def expert_kernel(
    n_row, n_sec, hot_ref, chosen_ref, weight_ref, x_hbm, cot_hbm, win_hbm, wout_hbm,
    shift_out, rows_out, scale_out, grad_out,
    x_v, cot_v, win_v, wout_v, gath, xs, gs, pack, land,
    scale_v, scale_land, score_v, score_land, zero_v,
    win_sem, wout_sem, t_sem, gath_send, gath_recv, back_send, back_recv, score_send, score_recv,
    small_send, small_recv, shift_send, shift_recv, zero_sem,
):
    sec = lax.axis_index("section")
    me = lax.axis_index("row")
    tokens, width = x_v.shape
    slots = n_row * CAP
    part = width // BANDS
    quarter = width // QUARTERS
    band = quarter // BANDS

    def win_copy(i, c):
        rows = pl.ds(c * quarter, quarter)
        return pltpu.make_async_copy(win_hbm.at[i, rows], win_v.at[i, rows], win_sem.at[i, c])

    wout_copy = pltpu.make_async_copy(wout_hbm, wout_v, wout_sem)
    x_copy = pltpu.make_async_copy(x_hbm, x_v, t_sem.at[0])
    cot_copy = pltpu.make_async_copy(cot_hbm, cot_v, t_sem.at[1])
    x_copy.start()
    cot_copy.start()

    has_prev = sec > 0
    has_next = sec < n_sec - 1
    barrier = pltpu.get_barrier_semaphore()

    @pl.loop(1, n_row)
    def _(i):
        pl.semaphore_signal(
            barrier, inc=1, device_id={"section": sec, "row": lax.rem(me + i, n_row)}, device_id_type=MESH
        )

    @pl.when(has_prev)
    def _():
        @pl.loop(0, n_row)
        def _(r):
            pl.semaphore_signal(barrier, inc=1, device_id={"section": sec - 1, "row": r}, device_id_type=MESH)

    @pl.when(has_next)
    def _():
        @pl.loop(0, n_row)
        def _(r):
            pl.semaphore_signal(barrier, inc=1, device_id={"section": sec + 1, "row": r}, device_id_type=MESH)

    hit = (chosen_ref[...] == hot_ref[0]).astype(F32)
    hit_tok = jnp.sum(hit, axis=0, keepdims=True)
    before = (iota((tokens, tokens), 0) < iota((tokens, tokens), 1)).astype(BF16)
    order = jnp.dot(
        jnp.broadcast_to(hit_tok, (ROWS, tokens)).astype(BF16), before, preferred_element_type=F32
    )[0:1]
    picks = [jnp.where(order == float(j), hit_tok, 0.0) for j in range(CAP)]
    held = hit * sum(picks)
    weight_tok = jnp.sum(held * weight_ref[...], axis=0, keepdims=True)
    row8 = iota((8, tokens), 0)
    scale = jnp.zeros((8, tokens), F32)
    for j in range(CAP):
        scale = scale + jnp.where(row8 == j, weight_tok * picks[j], 0.0)
    scale_v[...] = scale

    lead = iota((ROWS, tokens), 0)
    ones = []
    for c in range(BANDS):
        one = jnp.zeros((ROWS, tokens), F32)
        for j in range(CAP):
            one = one + jnp.where(lead == c * CAP + j, picks[j], 0.0)
        ones.append(one.astype(BF16))

    def held_rows(source):
        block = jnp.zeros((ROWS, part), F32)
        for c in range(BANDS):
            block = block + jnp.dot(
                ones[c], source[:, c * part : (c + 1) * part], preferred_element_type=F32
            )
        return block.astype(BF16)

    def gath_copy(k, to, slot_of):
        return pltpu.make_async_remote_copy(
            gath.at[k, slot_of], gath.at[k, slot_of], gath_send.at[k, to], gath_recv.at[k, slot_of],
            device_id={"section": sec, "row": to}, device_id_type=MESH,
        )

    prev = {"section": sec - 1, "row": me}
    shift = pltpu.make_async_remote_copy(
        cot_hbm, shift_out, shift_send, shift_recv, device_id=prev, device_id_type=MESH
    )
    small = pltpu.make_async_remote_copy(
        scale_v, scale_land, small_send, small_recv, device_id=prev, device_id_type=MESH
    )
    blank = pltpu.make_async_copy(zero_v, shift_out, zero_sem)

    x_copy.wait()
    gath[0, pl.ds(me, 1)] = held_rows(x_v)[None]

    sides = has_prev.astype(jnp.int32) + has_next.astype(jnp.int32)
    pl.semaphore_wait(barrier, n_row - 1 + n_row * sides)

    @pl.loop(1, n_row)
    def _(i):
        gath_copy(0, lax.rem(me + i, n_row), me).start()

    cot_copy.wait()
    for c in range(QUARTERS):
        win_copy(0, c).start()
        win_copy(1, c).start()
    wout_copy.start()

    gath[1, pl.ds(me, 1)] = held_rows(cot_v)[None]

    @pl.loop(1, n_row)
    def _(i):
        gath_copy(1, lax.rem(me + i, n_row), me).start()

    @pl.when(has_prev)
    def _():
        shift.start()
        small.start()

    @pl.when(jnp.logical_not(has_next))
    def _():
        zero_v[...] = jnp.zeros_like(zero_v)
        blank.start()

    to_row = iota((BANDS * slots, n_row * ROWS), 0)
    slot = lax.rem(to_row, slots)
    want = (slot // CAP) * ROWS + (to_row // slots) * CAP + lax.rem(slot, CAP)
    spread = (iota((BANDS * slots, n_row * ROWS), 1) == want).astype(BF16)

    def gathered(k, rows_ref):
        @pl.loop(1, n_row)
        def _(i):
            src = lax.rem(me + i, n_row)
            gath_copy(k, src, src).wait_recv()

        everyone = gath[k].reshape(n_row * ROWS, part)
        rows = jnp.dot(spread, everyone, preferred_element_type=F32).astype(BF16)
        for c in range(BANDS):
            rows_ref[:, c * part : (c + 1) * part] = rows[c * slots : (c + 1) * slots]

    gathered(0, xs)
    gate = up = None
    for c in range(QUARTERS):
        cols = slice(c * quarter, (c + 1) * quarter)
        win_copy(0, c).wait()
        win_copy(1, c).wait()
        g_part = jnp.dot(xs[:, cols], win_v[0, cols, :], preferred_element_type=F32)
        u_part = jnp.dot(xs[:, cols], win_v[1, cols, :], preferred_element_type=F32)
        gate = g_part if gate is None else gate + g_part
        up = u_part if up is None else up + u_part

    gathered(1, gs)
    wout_copy.wait()
    dh = lax.dot_general(wout_v[...], gs[...], LAST, preferred_element_type=F32).T

    sig = jax.nn.sigmoid(gate)
    hidden = (gate * sig * up).astype(BF16)
    dgate = (dh * up * sig * (1.0 + gate * (1.0 - sig))).astype(BF16)
    dup = (dh * gate * sig).astype(BF16)
    score = jnp.sum(hidden.astype(F32) * dh, axis=1, keepdims=True)
    diag = iota((slots, 128), 0) == iota((slots, 128), 1)
    score_row = jnp.sum(jnp.where(diag, score, 0.0), axis=0, keepdims=True)
    score_v[...] = jnp.broadcast_to(score_row, score_v.shape)

    def score_copy(to, slot_of):
        return pltpu.make_async_remote_copy(
            score_v, score_land.at[slot_of], score_send.at[to], score_recv.at[slot_of],
            device_id={"section": sec, "row": to}, device_id_type=MESH,
        )

    @pl.loop(1, n_row)
    def _(i):
        score_copy(lax.rem(me + i, n_row), me).start()

    score_land[pl.ds(me, 1)] = score_v[...][None]

    def back_copy(q, r, slot_of):
        return pltpu.make_async_remote_copy(
            pack.at[q, r], land.at[q, slot_of], back_send.at[q, r], back_recv.at[q, slot_of],
            device_id={"section": sec - 1, "row": r}, device_id_type=MESH,
        )

    @pl.when(has_prev)
    def _():
        out_row = iota((n_row * ROWS, BANDS * slots), 0)
        inner = lax.rem(out_row, ROWS)
        source = (inner // CAP) * slots + (out_row // ROWS) * CAP + lax.rem(inner, CAP)
        perm = (iota((n_row * ROWS, BANDS * slots), 1) == source).astype(BF16)
        for q in range(QUARTERS):
            rows = slice(q * quarter, (q + 1) * quarter)
            total = lax.dot_general(win_v[0, rows, :], dgate, LAST, preferred_element_type=F32)
            total = total + lax.dot_general(win_v[1, rows, :], dup, LAST, preferred_element_type=F32)
            back = total.T.astype(BF16)
            stack = jnp.concatenate([back[:, b * band : (b + 1) * band] for b in range(BANDS)], axis=0)
            packed = jnp.dot(perm, stack, preferred_element_type=F32).astype(BF16)
            pack[q] = packed.reshape(n_row, ROWS, band)

            @pl.loop(0, n_row)
            def _(r):
                back_copy(q, r, me).start()

    @pl.loop(1, n_row)
    def _(i):
        src = lax.rem(me + i, n_row)
        score_copy(src, src).wait_recv()

    sums = jnp.sum(score_land[...], axis=0)
    lane = iota(sums.shape, 1)
    grad_tok = jnp.zeros((1, tokens), F32)
    for j in range(CAP):
        mine = jnp.sum(jnp.where(lane == me * CAP + j, sums, 0.0), axis=1, keepdims=True)[0:1]
        grad_tok = grad_tok + picks[j] * mine
    grad_out[...] = held * grad_tok

    @pl.when(has_next)
    def _():
        small.wait_recv()
        diag = iota((tokens, tokens), 0) == iota((tokens, tokens), 1)
        for j in range(CAP):
            scale_out[:, j : j + 1] = jnp.sum(
                jnp.where(diag, scale_land[j : j + 1, :], 0.0), axis=1, keepdims=True
            )
        shift.wait_recv()
        for q in range(QUARTERS):
            @pl.loop(0, n_row)
            def _(r):
                back_copy(q, r, r).wait_recv()

            total = jnp.sum(land[q].astype(F32), axis=0).astype(BF16).astype(F32)
            for b in range(BANDS):
                at = q * quarter + b * band
                rows_out[:, at : at + band] = total[b * CAP : (b + 1) * CAP]

    @pl.when(jnp.logical_not(has_next))
    def _():
        rows_out[...] = jnp.zeros_like(rows_out)
        scale_out[...] = jnp.zeros_like(scale_out)
        blank.wait()

    @pl.loop(1, n_row)
    def _(i):
        to = lax.rem(me + i, n_row)
        gath_copy(0, to, me).wait_send()
        gath_copy(1, to, me).wait_send()
        score_copy(to, me).wait_send()

    @pl.when(has_prev)
    def _():
        shift.wait_send()
        small.wait_send()

        @pl.loop(0, n_row)
        def _(r):
            for q in range(QUARTERS):
                back_copy(q, r, me).wait_send()


def on_device(n_row, n_sec, layer_input, cotangent, route_weight, chosen, hot_expert, store_in, store_out):
    _, tokens, width = layer_input.shape
    ff = store_out.shape[1]
    top = chosen.shape[2]
    slots = n_row * CAP
    part = width // BANDS
    quarter = width // QUARTERS
    band = quarter // BANDS
    hbm = pl.BlockSpec(memory_space=pl.ANY)
    vmem = pl.BlockSpec(memory_space=pltpu.VMEM)
    dma = pltpu.SemaphoreType.DMA
    shift, rows, scale, grad = pl.pallas_call(
        functools.partial(expert_kernel, n_row, n_sec),
        out_shape=(
            pltpu.VMEM((tokens, width), BF16),
            pltpu.VMEM((CAP, width), F32),
            pltpu.VMEM((tokens, CAP), F32),
            pltpu.VMEM((top, tokens), F32),
        ),
        in_specs=[pl.BlockSpec(memory_space=pltpu.SMEM), vmem, vmem, hbm, hbm, hbm, hbm],
        out_specs=(vmem, vmem, vmem, vmem),
        scratch_shapes=[
            pltpu.VMEM((tokens, width), BF16),
            pltpu.VMEM((tokens, width), BF16),
            pltpu.VMEM((2, width, ff), BF16),
            pltpu.VMEM((ff, width), BF16),
            pltpu.VMEM((2, n_row, ROWS, part), BF16),
            pltpu.VMEM((slots, width), BF16),
            pltpu.VMEM((slots, width), BF16),
            pltpu.VMEM((QUARTERS, n_row, ROWS, band), BF16),
            pltpu.VMEM((QUARTERS, n_row, ROWS, band), BF16),
            pltpu.VMEM((8, tokens), F32),
            pltpu.VMEM((8, tokens), F32),
            pltpu.VMEM((8, 128), F32),
            pltpu.VMEM((n_row, 8, 128), F32),
            pltpu.VMEM((tokens, width), BF16),
            dma((2, QUARTERS)),
            dma,
            dma((2,)),
            dma((2, n_row)),
            dma((2, n_row)),
            dma((QUARTERS, n_row)),
            dma((QUARTERS, n_row)),
            dma((n_row,)),
            dma((n_row,)),
            dma,
            dma,
            dma,
            dma,
            dma,
        ],
        compiler_params=pltpu.CompilerParams(
            collective_id=0, has_side_effects=True, vmem_limit_bytes=60 * 2**20
        ),
        cost_estimate=pl.CostEstimate(
            flops=10 * slots * width * ff, bytes_accessed=6 * width * ff, transcendentals=slots * ff
        ),
        name="expert",
    )(
        hot_expert,
        jnp.transpose(chosen[0]),
        jnp.transpose(route_weight[0]),
        layer_input[0],
        cotangent[0],
        store_in[0],
        store_out[0],
    )
    moved = shift.astype(F32)
    for j in range(CAP):
        moved = moved + scale[:, j : j + 1] * rows[j : j + 1]
    moved = moved.astype(BF16)
    return (moved[None], jnp.transpose(grad)[None])


def token_select(block_c, hot, slot_count):
    count_tok, top_count = block_c.shape
    hit = (block_c == hot).astype(jnp.int32).reshape(-1)
    order = jnp.cumsum(hit) - hit
    held = hit * (order < slot_count).astype(jnp.int32)
    slots = (order[None, :] == jnp.arange(slot_count, dtype=jnp.int32)[:, None]).astype(
        jnp.int32
    ) * held[None, :]
    tsel = jnp.sum(slots.reshape(slot_count, count_tok, top_count), axis=2)
    return (tsel, held.reshape(count_tok, top_count))


def on_device_narrow(layer_input, cotangent, route_weight, chosen, hot_expert, store_in, store_out):
    tokens_here = layer_input[0]
    cot_here = cotangent[0]
    width = tokens_here.shape[1]
    num_row = lax.axis_size("row")
    size = lax.axis_size("section")
    tsel, held = token_select(chosen[0], hot_expert[0], CAP)
    pick = tsel.astype(BF16)
    rows = jnp.concatenate(
        [jnp.dot(pick, part, preferred_element_type=F32).astype(BF16) for part in (tokens_here, cot_here)], axis=1
    )
    both = lax.all_gather(rows, "row", axis=0, tiled=True)
    all_x, all_g = both[:, :width], both[:, width:]
    w_gate, w_up, w_out = store_in[0, 0], store_in[0, 1], store_out[0]
    gate = jnp.dot(all_x, w_gate, preferred_element_type=F32)
    upper = jnp.dot(all_x, w_up, preferred_element_type=F32)
    sig = jax.nn.sigmoid(gate)
    hidden = (gate * sig * upper).astype(BF16)
    d_hidden = lax.dot_general(all_g, w_out, LAST, preferred_element_type=F32)
    d_gate = (d_hidden * upper * sig * (1.0 + gate * (1.0 - sig))).astype(BF16)
    d_up = (d_hidden * gate * sig).astype(BF16)
    back_part = lax.dot_general(d_gate, w_gate, LAST, preferred_element_type=F32) + lax.dot_general(
        d_up, w_up, LAST, preferred_element_type=F32
    )
    score_part = jnp.sum(hidden.astype(F32) * d_hidden, axis=1)
    got_back = lax.all_to_all(
        back_part.reshape(num_row, CAP, width), "row", split_axis=0, concat_axis=0, tiled=True
    )
    got_score = lax.all_to_all(
        score_part.reshape(num_row, CAP), "row", split_axis=0, concat_axis=0, tiled=True
    )
    back_rows = jnp.sum(got_back, axis=0).astype(BF16)
    slot_score = jnp.sum(got_score, axis=0)
    back_tok = jnp.dot(pick.T, back_rows, preferred_element_type=F32)
    score_tok = jnp.sum(tsel.astype(F32).T * slot_score[None, :], axis=1)
    weight_tok = jnp.sum(held.astype(F32) * route_weight[0], axis=1)
    moved = (cot_here.astype(F32) + weight_tok[:, None] * back_tok).astype(BF16)
    route_grad = held.astype(F32) * score_tok[:, None]
    back_cot = lax.ppermute(moved, "section", [(i, i - 1) for i in range(1, size)])
    return (back_cot[None], route_grad[None])


def solution(mesh):
    n_row, n_sec = mesh.shape["row"], mesh.shape["section"]

    def body(layer_input, cotangent, route_weight, chosen, hot_expert, store_in, store_out):
        args = (layer_input, cotangent, route_weight, chosen, hot_expert, store_in, store_out)
        if store_out.shape[1] % 128 or n_row * CAP > 128:
            return on_device_narrow(*args)
        return on_device(n_row, n_sec, *args)

    in_specs = (
        P("section", "row", None),
        P("section", "row", None),
        P("section", "row", None),
        P("section", "row", None),
        P("section"),
        P("section", None, None, "row"),
        P("section", "row", None),
    )
    out_specs = (P("section", "row", None), P("section", "row", None))
    return jax.shard_map(body, mesh=mesh, in_specs=in_specs, out_specs=out_specs, check_vma=False)
```

```python
import functools

import jax
import jax.numpy as jnp
from jax import lax
from jax.experimental import pallas as pl
from jax.experimental.pallas import tpu as pltpu
from jax.sharding import PartitionSpec as P

CAP = 2
MESH = pl.DeviceIdType.MESH
F32 = jnp.float32
BF16 = jnp.bfloat16
ROWS = 16
BANDS = ROWS // CAP
QUARTERS = 4
LAST = (((1,), (1,)), ((), ()))
FIRST = (((0,), (1,)), ((), ()))


def iota(shape, dim):
    return lax.broadcasted_iota(jnp.int32, shape, dim)


def expert_kernel(
    n_row, n_sec, hot_ref, chosen_ref, weight_ref, x_hbm, cot_hbm, win_hbm, wout_hbm,
    shift_out, rows_out, scale_out, grad_out,
    x_v, cot_v, win_v, wout_v, gath, xs, gs, pack, land,
    scale_v, scale_land, score_v, score_land,
    win_sem, wout_sem, t_sem, gath_send, gath_recv, back_send, back_recv, score_send, score_recv,
    small_send, small_recv, shift_send, shift_recv,
):
    sec = lax.axis_index("section")
    me = lax.axis_index("row")
    tokens, width = x_v.shape
    slots = n_row * CAP
    part = width // BANDS
    quarter = width // QUARTERS
    band = quarter // BANDS

    def win_copy(i, c):
        rows = pl.ds(c * quarter, quarter)
        return pltpu.make_async_copy(win_hbm.at[i, rows], win_v.at[i, rows], win_sem.at[i, c])

    wout_copy = pltpu.make_async_copy(wout_hbm, wout_v, wout_sem)
    x_copy = pltpu.make_async_copy(x_hbm, x_v, t_sem.at[0])
    cot_copy = pltpu.make_async_copy(cot_hbm, cot_v, t_sem.at[1])
    x_copy.start()
    cot_copy.start()

    has_prev = sec > 0
    has_next = sec < n_sec - 1
    barrier = pltpu.get_barrier_semaphore()

    @pl.loop(1, n_row)
    def _(i):
        pl.semaphore_signal(
            barrier, inc=1, device_id={"section": sec, "row": lax.rem(me + i, n_row)}, device_id_type=MESH
        )

    @pl.when(has_prev)
    def _():
        @pl.loop(0, n_row)
        def _(r):
            pl.semaphore_signal(barrier, inc=1, device_id={"section": sec - 1, "row": r}, device_id_type=MESH)

    @pl.when(has_next)
    def _():
        @pl.loop(0, n_row)
        def _(r):
            pl.semaphore_signal(barrier, inc=1, device_id={"section": sec + 1, "row": r}, device_id_type=MESH)

    hit = (chosen_ref[...] == hot_ref[0]).astype(F32)
    hit_tok = jnp.sum(hit, axis=0, keepdims=True)
    before = (iota((tokens, tokens), 0) < iota((tokens, tokens), 1)).astype(BF16)
    order = jnp.dot(
        jnp.broadcast_to(hit_tok, (ROWS, tokens)).astype(BF16), before, preferred_element_type=F32
    )[0:1]
    picks = [jnp.where(order == float(j), hit_tok, 0.0) for j in range(CAP)]
    held = hit * sum(picks)
    weight_tok = jnp.sum(held * weight_ref[...], axis=0, keepdims=True)
    row8 = iota((8, tokens), 0)
    scale = jnp.zeros((8, tokens), F32)
    for j in range(CAP):
        scale = scale + jnp.where(row8 == j, weight_tok * picks[j], 0.0)
    scale_v[...] = scale

    lead = iota((ROWS, tokens), 0)
    ones = []
    for c in range(BANDS):
        one = jnp.zeros((ROWS, tokens), F32)
        for j in range(CAP):
            one = one + jnp.where(lead == c * CAP + j, picks[j], 0.0)
        ones.append(one.astype(BF16))

    def held_rows(source):
        block = jnp.zeros((ROWS, part), F32)
        for c in range(BANDS):
            block = block + jnp.dot(
                ones[c], source[:, c * part : (c + 1) * part], preferred_element_type=F32
            )
        return block.astype(BF16)

    def gath_copy(k, i):
        return pltpu.make_async_remote_copy(
            gath.at[k, 0], gath.at[k, i], gath_send.at[k], gath_recv.at[k],
            device_id={"section": sec, "row": lax.rem(me + n_row - i, n_row)}, device_id_type=MESH,
        )

    def gath_all(k):
        others = gath.at[k, pl.ds(1, n_row - 1)]
        return pltpu.make_async_remote_copy(
            others, others, gath_send.at[k], gath_recv.at[k],
            device_id={"section": sec, "row": me}, device_id_type=MESH,
        )

    prev = {"section": sec - 1, "row": me}
    shift = pltpu.make_async_remote_copy(
        cot_hbm, shift_out, shift_send, shift_recv, device_id=prev, device_id_type=MESH
    )
    small = pltpu.make_async_remote_copy(
        scale_v, scale_land, small_send, small_recv, device_id=prev, device_id_type=MESH
    )

    x_copy.wait()
    gath[0, 0] = held_rows(x_v)

    sides = has_prev.astype(jnp.int32) + has_next.astype(jnp.int32)
    pl.semaphore_wait(barrier, n_row - 1 + n_row * sides)

    @pl.loop(1, n_row)
    def _(i):
        gath_copy(0, i).start()

    cot_copy.wait()
    for c in range(QUARTERS):
        win_copy(0, c).start()
        win_copy(1, c).start()
    wout_copy.start()

    gath[1, 0] = held_rows(cot_v)

    @pl.loop(1, n_row)
    def _(i):
        gath_copy(1, i).start()

    @pl.when(has_prev)
    def _():
        shift.start()
        small.start()

    to_row = iota((BANDS * slots, n_row * ROWS), 0)
    slot = lax.rem(to_row, slots)
    away = lax.rem(slot // CAP - me + n_row, n_row)
    want = away * ROWS + (to_row // slots) * CAP + lax.rem(slot, CAP)
    spread = (iota((BANDS * slots, n_row * ROWS), 1) == want).astype(BF16)

    def gathered(k, rows_ref):
        gath_all(k).wait_recv()
        everyone = gath[k].reshape(n_row * ROWS, part)
        rows = jnp.dot(spread, everyone, preferred_element_type=F32).astype(BF16)
        for c in range(BANDS):
            rows_ref[:, c * part : (c + 1) * part] = rows[c * slots : (c + 1) * slots]

    gathered(0, xs)
    gate = up = None
    for c in range(QUARTERS):
        cols = slice(c * quarter, (c + 1) * quarter)
        win_copy(0, c).wait()
        win_copy(1, c).wait()
        g_part = lax.dot_general(win_v[0, cols, :], xs[:, cols], FIRST, preferred_element_type=F32)
        u_part = lax.dot_general(win_v[1, cols, :], xs[:, cols], FIRST, preferred_element_type=F32)
        gate = g_part if gate is None else gate + g_part
        up = u_part if up is None else up + u_part

    gate, up = gate.T, up.T
    gathered(1, gs)
    wout_copy.wait()
    dh = lax.dot_general(wout_v[...], gs[...], LAST, preferred_element_type=F32).T

    sig = jax.nn.sigmoid(gate)
    hidden = (gate * sig * up).astype(BF16)
    dgate = (dh * up * sig * (1.0 + gate * (1.0 - sig))).astype(BF16)
    dup = (dh * gate * sig).astype(BF16)
    score = jnp.sum(hidden.astype(F32) * dh, axis=1, keepdims=True)
    diag = iota((slots, 128), 0) == iota((slots, 128), 1)
    score_row = jnp.sum(jnp.where(diag, score, 0.0), axis=0, keepdims=True)
    score_v[...] = jnp.broadcast_to(score_row, score_v.shape)

    score_land[0] = score_v[...]

    def score_copy(i):
        return pltpu.make_async_remote_copy(
            score_v, score_land.at[i], score_send, score_recv,
            device_id={"section": sec, "row": lax.rem(me + n_row - i, n_row)}, device_id_type=MESH,
        )

    def score_all():
        others = score_land.at[pl.ds(1, n_row - 1)]
        return pltpu.make_async_remote_copy(
            others, others, score_send, score_recv,
            device_id={"section": sec, "row": me}, device_id_type=MESH,
        )

    @pl.loop(1, n_row)
    def _(i):
        score_copy(i).start()

    def back_copy(q, r):
        return pltpu.make_async_remote_copy(
            pack.at[q, r], land.at[q, me], back_send.at[q], back_recv.at[q],
            device_id={"section": sec - 1, "row": r}, device_id_type=MESH,
        )

    def back_all(q):
        return pltpu.make_async_remote_copy(
            pack.at[q], land.at[q], back_send.at[q], back_recv.at[q],
            device_id={"section": sec - 1, "row": me}, device_id_type=MESH,
        )

    @pl.when(has_prev)
    def _():
        out_row = iota((n_row * ROWS, BANDS * slots), 0)
        inner = lax.rem(out_row, ROWS)
        source = (inner // CAP) * slots + (out_row // ROWS) * CAP + lax.rem(inner, CAP)
        perm = (iota((n_row * ROWS, BANDS * slots), 1) == source).astype(BF16)
        for q in range(QUARTERS):
            rows = slice(q * quarter, (q + 1) * quarter)
            total = lax.dot_general(win_v[0, rows, :], dgate, LAST, preferred_element_type=F32)
            total = total + lax.dot_general(win_v[1, rows, :], dup, LAST, preferred_element_type=F32)
            back = total.T.astype(BF16)
            stack = jnp.concatenate([back[:, b * band : (b + 1) * band] for b in range(BANDS)], axis=0)
            packed = jnp.dot(perm, stack, preferred_element_type=F32).astype(BF16)
            pack[q] = packed.reshape(n_row, ROWS, band)

            @pl.loop(0, n_row)
            def _(r):
                back_copy(q, r).start()

    score_all().wait_recv()
    sums = jnp.sum(score_land[...], axis=0)
    lane = iota(sums.shape, 1)
    grad_tok = jnp.zeros((1, tokens), F32)
    for j in range(CAP):
        mine = jnp.sum(jnp.where(lane == me * CAP + j, sums, 0.0), axis=1, keepdims=True)[0:1]
        grad_tok = grad_tok + picks[j] * mine
    grad_out[...] = held * grad_tok

    gath_all(0).wait_send()
    gath_all(1).wait_send()
    score_all().wait_send()

    @pl.when(has_prev)
    def _():
        small.wait_send()
        shift.wait_send()

    @pl.when(has_next)
    def _():
        small.wait_recv()
        diag = iota((tokens, tokens), 0) == iota((tokens, tokens), 1)
        for j in range(CAP):
            col = jnp.sum(jnp.where(diag, scale_land[j : j + 1, :], 0.0), axis=1, keepdims=True)
            scale_out[j] = jnp.broadcast_to(col, (tokens, band))
        shift.wait_recv()
        for q in range(QUARTERS):
            back_all(q).wait_recv()
            rows_out[q] = jnp.sum(land[q].astype(F32), axis=0).astype(BF16).astype(F32)

    @pl.when(jnp.logical_not(has_next))
    def _():
        rows_out[...] = jnp.zeros_like(rows_out)
        scale_out[...] = jnp.zeros_like(scale_out)
        shift_out[...] = jnp.zeros_like(shift_out)

    @pl.when(has_prev)
    def _():
        for q in range(QUARTERS):
            back_all(q).wait_send()


def merge_kernel(shift_ref, rows_ref, scale_ref, grad_ref, out_hbm, grad_hbm, out_v, sem):
    quarters, _, band = rows_ref.shape
    quarter = band * BANDS
    grad_copy = pltpu.make_async_copy(grad_ref, grad_hbm, sem.at[quarters])
    grad_copy.start()
    copies = []
    for q in range(quarters):
        for b in range(BANDS):
            at = slice(q * quarter + b * band, q * quarter + (b + 1) * band)
            value = shift_ref[:, at].astype(F32)
            for j in range(CAP):
                value = value + scale_ref[j] * rows_ref[q, b * CAP + j : b * CAP + j + 1, :]
            out_v[:, at] = value.astype(BF16)
        cols = pl.ds(q * quarter, quarter)
        copies.append(pltpu.make_async_copy(out_v.at[:, cols], out_hbm.at[:, cols], sem.at[q]))
        copies[-1].start()
    for copy in copies:
        copy.wait()
    grad_copy.wait()


def on_device(n_row, n_sec, layer_input, cotangent, route_weight, chosen, hot_expert, store_in, store_out):
    _, tokens, width = layer_input.shape
    ff = store_out.shape[1]
    top = chosen.shape[2]
    slots = n_row * CAP
    part = width // BANDS
    quarter = width // QUARTERS
    band = quarter // BANDS
    hbm = pl.BlockSpec(memory_space=pl.ANY)
    vmem = pl.BlockSpec(memory_space=pltpu.VMEM)
    dma = pltpu.SemaphoreType.DMA
    shift, rows, scale, grad = pl.pallas_call(
        functools.partial(expert_kernel, n_row, n_sec),
        out_shape=(
            pltpu.VMEM((tokens, width), BF16),
            pltpu.VMEM((QUARTERS, ROWS, band), F32),
            pltpu.VMEM((CAP, tokens, band), F32),
            pltpu.VMEM((top, tokens), F32),
        ),
        in_specs=[pl.BlockSpec(memory_space=pltpu.SMEM), vmem, vmem, hbm, hbm, hbm, hbm],
        out_specs=(vmem, vmem, vmem, vmem),
        scratch_shapes=[
            pltpu.VMEM((tokens, width), BF16),
            pltpu.VMEM((tokens, width), BF16),
            pltpu.VMEM((2, width, ff), BF16),
            pltpu.VMEM((ff, width), BF16),
            pltpu.VMEM((2, n_row, ROWS, part), BF16),
            pltpu.VMEM((slots, width), BF16),
            pltpu.VMEM((slots, width), BF16),
            pltpu.VMEM((QUARTERS, n_row, ROWS, band), BF16),
            pltpu.VMEM((QUARTERS, n_row, ROWS, band), BF16),
            pltpu.VMEM((8, tokens), F32),
            pltpu.VMEM((8, tokens), F32),
            pltpu.VMEM((8, 128), F32),
            pltpu.VMEM((n_row, 8, 128), F32),
            dma((2, QUARTERS)),
            dma,
            dma((2,)),
            dma((2,)),
            dma((2,)),
            dma((QUARTERS,)),
            dma((QUARTERS,)),
            dma,
            dma,
            dma,
            dma,
            dma,
            dma,
        ],
        compiler_params=pltpu.CompilerParams(
            collective_id=0, has_side_effects=True, vmem_limit_bytes=60 * 2**20
        ),
        cost_estimate=pl.CostEstimate(
            flops=10 * slots * width * ff, bytes_accessed=6 * width * ff, transcendentals=slots * ff
        ),
        name="expert",
    )(
        hot_expert,
        jnp.transpose(chosen[0]),
        jnp.transpose(route_weight[0]),
        layer_input[0],
        cotangent[0],
        store_in[0],
        store_out[0],
    )
    moved, grad = pl.pallas_call(
        merge_kernel,
        out_shape=(
            jax.ShapeDtypeStruct((tokens, width), BF16),
            jax.ShapeDtypeStruct((top, tokens), F32),
        ),
        in_specs=[vmem] * 4,
        out_specs=(hbm, hbm),
        scratch_shapes=[pltpu.VMEM((tokens, width), BF16), dma((QUARTERS + 1,))],
        name="merge",
    )(shift, rows, scale, grad)
    return (moved[None], jnp.transpose(grad)[None])


def token_select(block_c, hot, slot_count):
    count_tok, top_count = block_c.shape
    hit = (block_c == hot).astype(jnp.int32).reshape(-1)
    order = jnp.cumsum(hit) - hit
    held = hit * (order < slot_count).astype(jnp.int32)
    slots = (order[None, :] == jnp.arange(slot_count, dtype=jnp.int32)[:, None]).astype(
        jnp.int32
    ) * held[None, :]
    tsel = jnp.sum(slots.reshape(slot_count, count_tok, top_count), axis=2)
    return (tsel, held.reshape(count_tok, top_count))


def on_device_narrow(layer_input, cotangent, route_weight, chosen, hot_expert, store_in, store_out):
    tokens_here = layer_input[0]
    cot_here = cotangent[0]
    width = tokens_here.shape[1]
    num_row = lax.axis_size("row")
    size = lax.axis_size("section")
    tsel, held = token_select(chosen[0], hot_expert[0], CAP)
    pick = tsel.astype(BF16)
    rows = jnp.concatenate(
        [jnp.dot(pick, part, preferred_element_type=F32).astype(BF16) for part in (tokens_here, cot_here)], axis=1
    )
    both = lax.all_gather(rows, "row", axis=0, tiled=True)
    all_x, all_g = both[:, :width], both[:, width:]
    w_gate, w_up, w_out = store_in[0, 0], store_in[0, 1], store_out[0]
    gate = jnp.dot(all_x, w_gate, preferred_element_type=F32)
    upper = jnp.dot(all_x, w_up, preferred_element_type=F32)
    sig = jax.nn.sigmoid(gate)
    hidden = (gate * sig * upper).astype(BF16)
    d_hidden = lax.dot_general(all_g, w_out, LAST, preferred_element_type=F32)
    d_gate = (d_hidden * upper * sig * (1.0 + gate * (1.0 - sig))).astype(BF16)
    d_up = (d_hidden * gate * sig).astype(BF16)
    back_part = lax.dot_general(d_gate, w_gate, LAST, preferred_element_type=F32) + lax.dot_general(
        d_up, w_up, LAST, preferred_element_type=F32
    )
    score_part = jnp.sum(hidden.astype(F32) * d_hidden, axis=1)
    got_back = lax.all_to_all(
        back_part.reshape(num_row, CAP, width), "row", split_axis=0, concat_axis=0, tiled=True
    )
    got_score = lax.all_to_all(
        score_part.reshape(num_row, CAP), "row", split_axis=0, concat_axis=0, tiled=True
    )
    back_rows = jnp.sum(got_back, axis=0).astype(BF16)
    slot_score = jnp.sum(got_score, axis=0)
    back_tok = jnp.dot(pick.T, back_rows, preferred_element_type=F32)
    score_tok = jnp.sum(tsel.astype(F32).T * slot_score[None, :], axis=1)
    weight_tok = jnp.sum(held.astype(F32) * route_weight[0], axis=1)
    moved = (cot_here.astype(F32) + weight_tok[:, None] * back_tok).astype(BF16)
    route_grad = held.astype(F32) * score_tok[:, None]
    back_cot = lax.ppermute(moved, "section", [(i, i - 1) for i in range(1, size)])
    return (back_cot[None], route_grad[None])


def solution(mesh):
    n_row, n_sec = mesh.shape["row"], mesh.shape["section"]

    def body(layer_input, cotangent, route_weight, chosen, hot_expert, store_in, store_out):
        args = (layer_input, cotangent, route_weight, chosen, hot_expert, store_in, store_out)
        if store_out.shape[1] % 128 or n_row * CAP > 128:
            return on_device_narrow(*args)
        return on_device(n_row, n_sec, *args)

    in_specs = (
        P("section", "row", None),
        P("section", "row", None),
        P("section", "row", None),
        P("section", "row", None),
        P("section"),
        P("section", None, None, "row"),
        P("section", "row", None),
    )
    out_specs = (P("section", "row", None), P("section", "row", None))
    return jax.shard_map(body, mesh=mesh, in_specs=in_specs, out_specs=out_specs, check_vma=False)
```

```python
import functools

import jax
import jax.numpy as jnp
from jax import lax
from jax.experimental import pallas as pl
from jax.experimental.pallas import tpu as pltpu
from jax.sharding import PartitionSpec as P

CAP = 2
MESH = pl.DeviceIdType.MESH
F32 = jnp.float32
BF16 = jnp.bfloat16
ROWS = 16
BANDS = ROWS // CAP
QUARTERS = 4
HALVES = 2
LAST = (((1,), (1,)), ((), ()))


def iota(shape, dim):
    return lax.broadcasted_iota(jnp.int32, shape, dim)


def expert_kernel(
    n_row, n_sec, hot_ref, chosen_ref, weight_ref, x_hbm, cot_hbm, win_hbm, wout_hbm,
    moved_out, grad_out,
    x_v, cot_v, win_v, wout_v, gath, xs, gs, pack, land,
    scale_v, scale_land, score_v, score_land,
    win_sem, wout_sem, t_sem, gath_send, gath_recv, back_send, back_recv, score_send, score_recv,
    small_send, small_recv, shift_send, shift_recv,
):
    sec = lax.axis_index("section")
    me = lax.axis_index("row")
    tokens, width = x_v.shape
    slots = n_row * CAP
    half = width // HALVES
    part = half // BANDS
    quarter = width // QUARTERS
    band = quarter // BANDS

    def win_copy(i, c):
        rows = pl.ds(c * quarter, quarter)
        return pltpu.make_async_copy(win_hbm.at[i, rows], win_v.at[i, rows], win_sem.at[i, c])

    wout_copy = pltpu.make_async_copy(wout_hbm, wout_v, wout_sem)
    def token_copy(k):
        source, to = ((x_hbm, x_v), (cot_hbm, cot_v))[k // HALVES]
        cols = pl.ds(k % HALVES * half, half)
        return pltpu.make_async_copy(source.at[:, cols], to.at[:, cols], t_sem.at[k])

    for k in range(2 * HALVES):
        token_copy(k).start()

    has_prev = sec > 0
    has_next = sec < n_sec - 1
    barrier = pltpu.get_barrier_semaphore()

    @pl.loop(1, n_row)
    def _(i):
        pl.semaphore_signal(
            barrier, inc=1, device_id={"section": sec, "row": lax.rem(me + i, n_row)}, device_id_type=MESH
        )

    @pl.when(has_prev)
    def _():
        @pl.loop(0, n_row)
        def _(r):
            pl.semaphore_signal(barrier, inc=1, device_id={"section": sec - 1, "row": r}, device_id_type=MESH)

    @pl.when(has_next)
    def _():
        @pl.loop(0, n_row)
        def _(r):
            pl.semaphore_signal(barrier, inc=1, device_id={"section": sec + 1, "row": r}, device_id_type=MESH)

    hit = (chosen_ref[...] == hot_ref[0]).astype(F32)
    hit_tok = jnp.sum(hit, axis=0, keepdims=True)
    before = (iota((tokens, tokens), 0) < iota((tokens, tokens), 1)).astype(BF16)
    order = jnp.dot(
        jnp.broadcast_to(hit_tok, (ROWS, tokens)).astype(BF16), before, preferred_element_type=F32
    )[0:1]
    picks = [jnp.where(order == float(j), hit_tok, 0.0) for j in range(CAP)]
    held = hit * sum(picks)
    weight_tok = jnp.sum(held * weight_ref[...], axis=0, keepdims=True)
    row8 = iota((8, tokens), 0)
    scale = jnp.zeros((8, tokens), F32)
    for j in range(CAP):
        scale = scale + jnp.where(row8 == j, weight_tok * picks[j], 0.0)
    scale_v[...] = scale

    lead = iota((ROWS, tokens), 0)
    ones = []
    for c in range(BANDS):
        one = jnp.zeros((ROWS, tokens), F32)
        for j in range(CAP):
            one = one + jnp.where(lead == c * CAP + j, picks[j], 0.0)
        ones.append(one.astype(BF16))

    def held_rows(k):
        source = (x_v, cot_v)[k // HALVES]
        block = jnp.zeros((ROWS, part), F32)
        for c in range(BANDS):
            at = k % HALVES * half + c * part
            block = block + jnp.dot(ones[c], source[:, at : at + part], preferred_element_type=F32)
        gath[k, 0] = block.astype(BF16)

    def send_rows(k):
        @pl.loop(1, n_row)
        def _(i):
            gath_copy(k, i).start()

    def gath_copy(k, i):
        return pltpu.make_async_remote_copy(
            gath.at[k, 0], gath.at[k, i], gath_send.at[k], gath_recv.at[k],
            device_id={"section": sec, "row": lax.rem(me + n_row - i, n_row)}, device_id_type=MESH,
        )

    def gath_all(k):
        others = gath.at[k, pl.ds(1, n_row - 1)]
        return pltpu.make_async_remote_copy(
            others, others, gath_send.at[k], gath_recv.at[k],
            device_id={"section": sec, "row": me}, device_id_type=MESH,
        )

    prev = {"section": sec - 1, "row": me}
    shift = pltpu.make_async_remote_copy(
        cot_hbm, moved_out, shift_send, shift_recv, device_id=prev, device_id_type=MESH
    )
    small = pltpu.make_async_remote_copy(
        scale_v, scale_land, small_send, small_recv, device_id=prev, device_id_type=MESH
    )

    token_copy(0).wait()
    held_rows(0)
    sides = has_prev.astype(jnp.int32) + has_next.astype(jnp.int32)
    pl.semaphore_wait(barrier, n_row - 1 + n_row * sides)
    send_rows(0)
    token_copy(1).wait()
    held_rows(1)
    send_rows(1)

    for k in range(HALVES, 2 * HALVES):
        token_copy(k).wait()
    for c in range(QUARTERS):
        win_copy(0, c).start()
        win_copy(1, c).start()
    wout_copy.start()

    for k in range(HALVES, 2 * HALVES):
        held_rows(k)
        send_rows(k)

    @pl.when(has_prev)
    def _():
        shift.start()
        small.start()

    to_row = iota((BANDS * slots, n_row * ROWS), 0)
    slot = lax.rem(to_row, slots)
    away = lax.rem(slot // CAP - me + n_row, n_row)
    want = away * ROWS + (to_row // slots) * CAP + lax.rem(slot, CAP)
    spread = (iota((BANDS * slots, n_row * ROWS), 1) == want).astype(BF16)

    def gathered(k, rows_ref, h):
        gath_all(k).wait_recv()
        everyone = gath[k].reshape(n_row * ROWS, part)
        rows = jnp.dot(spread, everyone, preferred_element_type=F32).astype(BF16)
        for c in range(BANDS):
            at = h * half + c * part
            rows_ref[:, at : at + part] = rows[c * slots : (c + 1) * slots]

    gate = up = None
    for c in range(QUARTERS):
        cols = slice(c * quarter, (c + 1) * quarter)
        if c % (QUARTERS // HALVES) == 0:
            gathered(c // (QUARTERS // HALVES), xs, c // (QUARTERS // HALVES))
        win_copy(0, c).wait()
        win_copy(1, c).wait()
        g_part = jnp.dot(xs[:, cols], win_v[0, cols, :], preferred_element_type=F32)
        u_part = jnp.dot(xs[:, cols], win_v[1, cols, :], preferred_element_type=F32)
        gate = g_part if gate is None else gate + g_part
        up = u_part if up is None else up + u_part

    gathered(2, gs, 0)
    gathered(3, gs, 1)
    wout_copy.wait()
    dh = lax.dot_general(wout_v[...], gs[...], LAST, preferred_element_type=F32).T

    sig = jax.nn.sigmoid(gate)
    hidden = (gate * sig * up).astype(BF16)
    dgate = (dh * up * sig * (1.0 + gate * (1.0 - sig))).astype(BF16)
    dup = (dh * gate * sig).astype(BF16)
    score = jnp.sum(hidden.astype(F32) * dh, axis=1, keepdims=True)
    diag = iota((slots, 128), 0) == iota((slots, 128), 1)
    score_row = jnp.sum(jnp.where(diag, score, 0.0), axis=0, keepdims=True)
    score_v[...] = jnp.broadcast_to(score_row, score_v.shape)

    score_land[0] = score_v[...]

    def score_copy(i):
        return pltpu.make_async_remote_copy(
            score_v, score_land.at[i], score_send, score_recv,
            device_id={"section": sec, "row": lax.rem(me + n_row - i, n_row)}, device_id_type=MESH,
        )

    def score_all():
        others = score_land.at[pl.ds(1, n_row - 1)]
        return pltpu.make_async_remote_copy(
            others, others, score_send, score_recv,
            device_id={"section": sec, "row": me}, device_id_type=MESH,
        )

    @pl.loop(1, n_row)
    def _(i):
        score_copy(i).start()

    def back_copy(q, r):
        return pltpu.make_async_remote_copy(
            pack.at[q, r], land.at[q, me], back_send.at[q], back_recv.at[q],
            device_id={"section": sec - 1, "row": r}, device_id_type=MESH,
        )

    def back_all(q):
        return pltpu.make_async_remote_copy(
            pack.at[q], land.at[q], back_send.at[q], back_recv.at[q],
            device_id={"section": sec - 1, "row": me}, device_id_type=MESH,
        )

    @pl.when(has_prev)
    def _():
        out_row = iota((n_row * ROWS, BANDS * slots), 0)
        inner = lax.rem(out_row, ROWS)
        source = (inner // CAP) * slots + (out_row // ROWS) * CAP + lax.rem(inner, CAP)
        perm = (iota((n_row * ROWS, BANDS * slots), 1) == source).astype(BF16)
        for q in range(QUARTERS):
            rows = slice(q * quarter, (q + 1) * quarter)
            total = lax.dot_general(win_v[0, rows, :], dgate, LAST, preferred_element_type=F32)
            total = total + lax.dot_general(win_v[1, rows, :], dup, LAST, preferred_element_type=F32)
            back = total.T.astype(BF16)
            stack = jnp.concatenate([back[:, b * band : (b + 1) * band] for b in range(BANDS)], axis=0)
            packed = jnp.dot(perm, stack, preferred_element_type=F32).astype(BF16)
            pack[q] = packed.reshape(n_row, ROWS, band)

            @pl.loop(0, n_row)
            def _(i):
                back_copy(q, lax.rem(me + i, n_row)).start()

    score_all().wait_recv()
    sums = jnp.sum(score_land[...], axis=0)
    lane = iota(sums.shape, 1)
    grad_tok = jnp.zeros((1, tokens), F32)
    for j in range(CAP):
        mine = jnp.sum(jnp.where(lane == me * CAP + j, sums, 0.0), axis=1, keepdims=True)[0:1]
        grad_tok = grad_tok + picks[j] * mine
    grad_out[...] = held * grad_tok

    for k in range(2 * HALVES):
        gath_all(k).wait_send()
    score_all().wait_send()

    @pl.when(has_prev)
    def _():
        small.wait_send()
        shift.wait_send()

    @pl.when(has_next)
    def _():
        small.wait_recv()
        diag = iota((tokens, tokens), 0) == iota((tokens, tokens), 1)
        scales = []
        for j in range(CAP):
            col = jnp.sum(jnp.where(diag, scale_land[j : j + 1, :], 0.0), axis=1, keepdims=True)
            scales.append(jnp.broadcast_to(col, (tokens, band)))
        shift.wait_recv()
        for q in range(QUARTERS):
            back_all(q).wait_recv()
            rows = jnp.sum(land[q].astype(F32), axis=0).astype(BF16).astype(F32)
            for b in range(BANDS):
                at = slice(q * quarter + b * band, q * quarter + (b + 1) * band)
                value = moved_out[:, at].astype(F32)
                for j in range(CAP):
                    value = value + scales[j] * rows[b * CAP + j : b * CAP + j + 1, :]
                moved_out[:, at] = value.astype(BF16)

    @pl.when(jnp.logical_not(has_next))
    def _():
        moved_out[...] = jnp.zeros_like(moved_out)

    @pl.when(has_prev)
    def _():
        for q in range(QUARTERS):
            back_all(q).wait_send()


def on_device(n_row, n_sec, layer_input, cotangent, route_weight, chosen, hot_expert, store_in, store_out):
    _, tokens, width = layer_input.shape
    ff = store_out.shape[1]
    top = chosen.shape[2]
    slots = n_row * CAP
    half = width // HALVES
    part = half // BANDS
    quarter = width // QUARTERS
    band = quarter // BANDS
    hbm = pl.BlockSpec(memory_space=pl.ANY)
    vmem = pl.BlockSpec(memory_space=pltpu.VMEM)
    dma = pltpu.SemaphoreType.DMA
    moved, grad = pl.pallas_call(
        functools.partial(expert_kernel, n_row, n_sec),
        out_shape=(
            pltpu.VMEM((tokens, width), BF16),
            pltpu.VMEM((top, tokens), F32),
        ),
        in_specs=[pl.BlockSpec(memory_space=pltpu.SMEM), vmem, vmem, hbm, hbm, hbm, hbm],
        out_specs=(vmem, vmem),
        scratch_shapes=[
            pltpu.VMEM((tokens, width), BF16),
            pltpu.VMEM((tokens, width), BF16),
            pltpu.VMEM((2, width, ff), BF16),
            pltpu.VMEM((ff, width), BF16),
            pltpu.VMEM((2 * HALVES, n_row, ROWS, part), BF16),
            pltpu.VMEM((slots, width), BF16),
            pltpu.VMEM((slots, width), BF16),
            pltpu.VMEM((QUARTERS, n_row, ROWS, band), BF16),
            pltpu.VMEM((QUARTERS, n_row, ROWS, band), BF16),
            pltpu.VMEM((8, tokens), F32),
            pltpu.VMEM((8, tokens), F32),
            pltpu.VMEM((8, 128), F32),
            pltpu.VMEM((n_row, 8, 128), F32),
            dma((2, QUARTERS)),
            dma,
            dma((2 * HALVES,)),
            dma((2 * HALVES,)),
            dma((2 * HALVES,)),
            dma((QUARTERS,)),
            dma((QUARTERS,)),
            dma,
            dma,
            dma,
            dma,
            dma,
            dma,
        ],
        compiler_params=pltpu.CompilerParams(
            collective_id=0, has_side_effects=True, vmem_limit_bytes=60 * 2**20
        ),
        cost_estimate=pl.CostEstimate(
            flops=10 * slots * width * ff, bytes_accessed=6 * width * ff, transcendentals=slots * ff
        ),
        name="expert",
    )(
        hot_expert,
        jnp.transpose(chosen[0]),
        jnp.transpose(route_weight[0]),
        layer_input[0],
        cotangent[0],
        store_in[0],
        store_out[0],
    )
    return (moved[None], jnp.transpose(grad)[None])


def token_select(block_c, hot, slot_count):
    count_tok, top_count = block_c.shape
    hit = (block_c == hot).astype(jnp.int32).reshape(-1)
    order = jnp.cumsum(hit) - hit
    held = hit * (order < slot_count).astype(jnp.int32)
    slots = (order[None, :] == jnp.arange(slot_count, dtype=jnp.int32)[:, None]).astype(
        jnp.int32
    ) * held[None, :]
    tsel = jnp.sum(slots.reshape(slot_count, count_tok, top_count), axis=2)
    return (tsel, held.reshape(count_tok, top_count))


def on_device_narrow(layer_input, cotangent, route_weight, chosen, hot_expert, store_in, store_out):
    tokens_here = layer_input[0]
    cot_here = cotangent[0]
    width = tokens_here.shape[1]
    num_row = lax.axis_size("row")
    size = lax.axis_size("section")
    tsel, held = token_select(chosen[0], hot_expert[0], CAP)
    pick = tsel.astype(BF16)
    rows = jnp.concatenate(
        [jnp.dot(pick, part, preferred_element_type=F32).astype(BF16) for part in (tokens_here, cot_here)], axis=1
    )
    both = lax.all_gather(rows, "row", axis=0, tiled=True)
    all_x, all_g = both[:, :width], both[:, width:]
    w_gate, w_up, w_out = store_in[0, 0], store_in[0, 1], store_out[0]
    gate = jnp.dot(all_x, w_gate, preferred_element_type=F32)
    upper = jnp.dot(all_x, w_up, preferred_element_type=F32)
    sig = jax.nn.sigmoid(gate)
    hidden = (gate * sig * upper).astype(BF16)
    d_hidden = lax.dot_general(all_g, w_out, LAST, preferred_element_type=F32)
    d_gate = (d_hidden * upper * sig * (1.0 + gate * (1.0 - sig))).astype(BF16)
    d_up = (d_hidden * gate * sig).astype(BF16)
    back_part = lax.dot_general(d_gate, w_gate, LAST, preferred_element_type=F32) + lax.dot_general(
        d_up, w_up, LAST, preferred_element_type=F32
    )
    score_part = jnp.sum(hidden.astype(F32) * d_hidden, axis=1)
    got_back = lax.all_to_all(
        back_part.reshape(num_row, CAP, width), "row", split_axis=0, concat_axis=0, tiled=True
    )
    got_score = lax.all_to_all(
        score_part.reshape(num_row, CAP), "row", split_axis=0, concat_axis=0, tiled=True
    )
    back_rows = jnp.sum(got_back, axis=0).astype(BF16)
    slot_score = jnp.sum(got_score, axis=0)
    back_tok = jnp.dot(pick.T, back_rows, preferred_element_type=F32)
    score_tok = jnp.sum(tsel.astype(F32).T * slot_score[None, :], axis=1)
    weight_tok = jnp.sum(held.astype(F32) * route_weight[0], axis=1)
    moved = (cot_here.astype(F32) + weight_tok[:, None] * back_tok).astype(BF16)
    route_grad = held.astype(F32) * score_tok[:, None]
    back_cot = lax.ppermute(moved, "section", [(i, i - 1) for i in range(1, size)])
    return (back_cot[None], route_grad[None])


def solution(mesh):
    n_row, n_sec = mesh.shape["row"], mesh.shape["section"]

    def body(layer_input, cotangent, route_weight, chosen, hot_expert, store_in, store_out):
        args = (layer_input, cotangent, route_weight, chosen, hot_expert, store_in, store_out)
        if store_out.shape[1] % 128 or n_row * CAP > 128:
            return on_device_narrow(*args)
        return on_device(n_row, n_sec, *args)

    in_specs = (
        P("section", "row", None),
        P("section", "row", None),
        P("section", "row", None),
        P("section", "row", None),
        P("section"),
        P("section", None, None, "row"),
        P("section", "row", None),
    )
    out_specs = (P("section", "row", None), P("section", "row", None))
    return jax.shard_map(body, mesh=mesh, in_specs=in_specs, out_specs=out_specs, check_vma=False)
```

```python
import functools

import jax
import jax.numpy as jnp
from jax import lax
from jax.experimental import pallas as pl
from jax.experimental.pallas import tpu as pltpu
from jax.sharding import PartitionSpec as P

CAP = 2
MESH = pl.DeviceIdType.MESH
F32 = jnp.float32
BF16 = jnp.bfloat16
ROWS = 16
BANDS = ROWS // CAP
QUARTERS = 4
HALVES = 2
LAST = (((1,), (1,)), ((), ()))


def iota(shape, dim):
    return lax.broadcasted_iota(jnp.int32, shape, dim)


def expert_kernel(
    n_row, n_sec, hot_ref, chosen_hbm, weight_hbm, x_hbm, cot_hbm, win_hbm, wout_hbm,
    moved_out, grad_out,
    chosen_ref, weight_ref, x_v, cot_v, win_v, wout_v, gath, xs, gs, pack, land,
    scale_v, scale_land, score_v, score_land,
    win_sem, wout_sem, pick_sem, t_sem, gath_send, gath_recv, back_send, back_recv, score_send, score_recv,
    small_send, small_recv, shift_send, shift_recv,
):
    sec = lax.axis_index("section")
    me = lax.axis_index("row")
    tokens, width = x_v.shape
    ff = wout_v.shape[0]
    slots = n_row * CAP
    half = width // HALVES
    part = half // BANDS
    quarter = width // QUARTERS
    band = quarter // BANDS

    def win_copy(i, c):
        rows = pl.ds(c * quarter, quarter)
        return pltpu.make_async_copy(
            win_hbm.at[i, rows], win_v.at[rows, pl.ds(i * ff, ff)], win_sem.at[i, c]
        )

    wout_copy = pltpu.make_async_copy(wout_hbm, wout_v, wout_sem)
    def token_copy(k):
        source, to = ((x_hbm, x_v), (cot_hbm, cot_v))[k // HALVES]
        cols = pl.ds(k % HALVES * half, half)
        return pltpu.make_async_copy(source.at[:, cols], to.at[:, cols], t_sem.at[k])

    pick_copies = [
        pltpu.make_async_copy(source, to, pick_sem.at[i])
        for i, (source, to) in enumerate(
            ((chosen_hbm, chosen_ref), (weight_hbm, weight_ref))
        )
    ]
    for copy in pick_copies:
        copy.start()
    for k in range(2 * HALVES):
        token_copy(k).start()

    has_prev = sec > 0
    has_next = sec < n_sec - 1
    barrier = pltpu.get_barrier_semaphore()

    @pl.loop(1, n_row)
    def _(i):
        pl.semaphore_signal(
            barrier, inc=1, device_id={"section": sec, "row": lax.rem(me + i, n_row)}, device_id_type=MESH
        )

    @pl.when(has_prev)
    def _():
        @pl.loop(0, n_row)
        def _(r):
            pl.semaphore_signal(barrier, inc=1, device_id={"section": sec - 1, "row": r}, device_id_type=MESH)

    @pl.when(has_next)
    def _():
        @pl.loop(0, n_row)
        def _(r):
            pl.semaphore_signal(barrier, inc=1, device_id={"section": sec + 1, "row": r}, device_id_type=MESH)

    for copy in pick_copies:
        copy.wait()

    hit = (chosen_ref[...] == hot_ref[0]).astype(F32)
    hit_tok = jnp.sum(hit, axis=0, keepdims=True)
    before = (iota((tokens, tokens), 0) < iota((tokens, tokens), 1)).astype(BF16)
    order = jnp.dot(
        jnp.broadcast_to(hit_tok, (ROWS, tokens)).astype(BF16), before, preferred_element_type=F32
    )[0:1]
    picks = [jnp.where(order == float(j), hit_tok, 0.0) for j in range(CAP)]
    held = hit * sum(picks)
    weight_tok = jnp.sum(held * weight_ref[...], axis=0, keepdims=True)
    row8 = iota((8, tokens), 0)
    scale = jnp.zeros((8, tokens), F32)
    for j in range(CAP):
        scale = scale + jnp.where(row8 == j, weight_tok * picks[j], 0.0)
    scale_v[...] = scale

    lead = iota((ROWS, tokens), 0)
    ones = []
    for c in range(BANDS):
        one = jnp.zeros((ROWS, tokens), F32)
        for j in range(CAP):
            one = one + jnp.where(lead == c * CAP + j, picks[j], 0.0)
        ones.append(one.astype(BF16))

    def held_rows(k):
        source = (x_v, cot_v)[k // HALVES]
        block = jnp.zeros((ROWS, part), F32)
        for c in range(BANDS):
            at = k % HALVES * half + c * part
            block = block + jnp.dot(ones[c], source[:, at : at + part], preferred_element_type=F32)
        gath[k, 0] = block.astype(BF16)

    def send_rows(k):
        @pl.loop(1, n_row)
        def _(i):
            gath_copy(k, i).start()

    def gath_copy(k, i):
        return pltpu.make_async_remote_copy(
            gath.at[k, 0], gath.at[k, i], gath_send.at[k], gath_recv.at[k],
            device_id={"section": sec, "row": lax.rem(me + n_row - i, n_row)}, device_id_type=MESH,
        )

    def gath_all(k):
        others = gath.at[k, pl.ds(1, n_row - 1)]
        return pltpu.make_async_remote_copy(
            others, others, gath_send.at[k], gath_recv.at[k],
            device_id={"section": sec, "row": me}, device_id_type=MESH,
        )

    prev = {"section": sec - 1, "row": me}
    shift = pltpu.make_async_remote_copy(
        cot_hbm, moved_out, shift_send, shift_recv, device_id=prev, device_id_type=MESH
    )
    small = pltpu.make_async_remote_copy(
        scale_v, scale_land, small_send, small_recv, device_id=prev, device_id_type=MESH
    )

    token_copy(0).wait()
    held_rows(0)
    sides = has_prev.astype(jnp.int32) + has_next.astype(jnp.int32)
    pl.semaphore_wait(barrier, n_row - 1 + n_row * sides)
    send_rows(0)
    token_copy(1).wait()
    held_rows(1)
    send_rows(1)

    for k in range(HALVES, 2 * HALVES):
        token_copy(k).wait()
    for c in range(QUARTERS):
        win_copy(0, c).start()
        win_copy(1, c).start()
    wout_copy.start()

    for k in range(HALVES, 2 * HALVES):
        held_rows(k)
        send_rows(k)

    @pl.when(has_prev)
    def _():
        shift.start()
        small.start()

    to_row = iota((BANDS * slots, n_row * ROWS), 0)
    slot = lax.rem(to_row, slots)
    away = lax.rem(slot // CAP - me + n_row, n_row)
    want = away * ROWS + (to_row // slots) * CAP + lax.rem(slot, CAP)
    spread = (iota((BANDS * slots, n_row * ROWS), 1) == want).astype(BF16)

    def gathered(k, rows_ref, h):
        gath_all(k).wait_recv()
        everyone = gath[k].reshape(n_row * ROWS, part)
        rows = jnp.dot(spread, everyone, preferred_element_type=F32).astype(BF16)
        for c in range(BANDS):
            at = h * half + c * part
            rows_ref[:, at : at + part] = rows[c * slots : (c + 1) * slots]

    both = jnp.zeros((slots, 2 * ff), F32)
    per = QUARTERS // HALVES
    for h in range(HALVES):
        gathered(h, xs, h)
        for c in range(h * per, (h + 1) * per):
            win_copy(0, c).wait()
            win_copy(1, c).wait()
        cols = slice(h * half, (h + 1) * half)
        both = both + jnp.dot(xs[:, cols], win_v[cols, :], preferred_element_type=F32)
    gate, up = both[:, :ff], both[:, ff:]

    gathered(2, gs, 0)
    gathered(3, gs, 1)
    wout_copy.wait()
    dh = lax.dot_general(wout_v[...], gs[...], LAST, preferred_element_type=F32).T

    sig = jax.nn.sigmoid(gate)
    hidden = (gate * sig * up).astype(BF16)
    dgate = (dh * up * sig * (1.0 + gate * (1.0 - sig))).astype(BF16)
    dup = (dh * gate * sig).astype(BF16)
    score = jnp.sum(hidden.astype(F32) * dh, axis=1, keepdims=True)
    diag = iota((slots, 128), 0) == iota((slots, 128), 1)
    score_row = jnp.sum(jnp.where(diag, score, 0.0), axis=0, keepdims=True)
    score_v[...] = jnp.broadcast_to(score_row, score_v.shape)

    score_land[0] = score_v[...]

    def score_copy(i):
        return pltpu.make_async_remote_copy(
            score_v, score_land.at[i], score_send, score_recv,
            device_id={"section": sec, "row": lax.rem(me + n_row - i, n_row)}, device_id_type=MESH,
        )

    def score_all():
        others = score_land.at[pl.ds(1, n_row - 1)]
        return pltpu.make_async_remote_copy(
            others, others, score_send, score_recv,
            device_id={"section": sec, "row": me}, device_id_type=MESH,
        )

    @pl.loop(1, n_row)
    def _(i):
        score_copy(i).start()

    def back_copy(q, r):
        return pltpu.make_async_remote_copy(
            pack.at[q, r], land.at[q, me], back_send.at[q], back_recv.at[q],
            device_id={"section": sec - 1, "row": r}, device_id_type=MESH,
        )

    def back_all(q):
        return pltpu.make_async_remote_copy(
            pack.at[q], land.at[q], back_send.at[q], back_recv.at[q],
            device_id={"section": sec - 1, "row": me}, device_id_type=MESH,
        )

    @pl.when(has_prev)
    def _():
        out_row = iota((n_row * ROWS, BANDS * slots), 0)
        inner = lax.rem(out_row, ROWS)
        source = (inner // CAP) * slots + (out_row // ROWS) * CAP + lax.rem(inner, CAP)
        perm = (iota((n_row * ROWS, BANDS * slots), 1) == source).astype(BF16)
        sides_d = jnp.concatenate([dgate, dup], axis=1)

        def product(q):
            rows = slice(q * quarter, (q + 1) * quarter)
            return lax.dot_general(win_v[rows, :], sides_d, LAST, preferred_element_type=F32)

        later = product(0)
        for q in range(QUARTERS):
            total = later
            if q + 1 < QUARTERS:
                later = product(q + 1)
            back = total.T.astype(BF16)
            stack = jnp.concatenate([back[:, b * band : (b + 1) * band] for b in range(BANDS)], axis=0)
            packed = jnp.dot(perm, stack, preferred_element_type=F32).astype(BF16)
            pack[q] = packed.reshape(n_row, ROWS, band)

            @pl.loop(0, n_row)
            def _(i):
                back_copy(q, lax.rem(me + i, n_row)).start()

    score_all().wait_recv()
    sums = jnp.sum(score_land[...], axis=0)
    lane = iota(sums.shape, 1)
    grad_tok = jnp.zeros((1, tokens), F32)
    for j in range(CAP):
        mine = jnp.sum(jnp.where(lane == me * CAP + j, sums, 0.0), axis=1, keepdims=True)[0:1]
        grad_tok = grad_tok + picks[j] * mine
    grad_out[...] = held * grad_tok

    for k in range(2 * HALVES):
        gath_all(k).wait_send()
    score_all().wait_send()

    @pl.when(has_prev)
    def _():
        small.wait_send()
        shift.wait_send()

    @pl.when(has_next)
    def _():
        small.wait_recv()
        diag = iota((tokens, tokens), 0) == iota((tokens, tokens), 1)
        scales = []
        for j in range(CAP):
            col = jnp.sum(jnp.where(diag, scale_land[j : j + 1, :], 0.0), axis=1, keepdims=True)
            scales.append(jnp.broadcast_to(col, (tokens, band)))
        shift.wait_recv()
        for q in range(QUARTERS):
            back_all(q).wait_recv()
            rows = jnp.sum(land[q].astype(F32), axis=0).astype(BF16).astype(F32)
            for b in range(BANDS):
                at = slice(q * quarter + b * band, q * quarter + (b + 1) * band)
                value = moved_out[:, at].astype(F32)
                for j in range(CAP):
                    value = value + scales[j] * rows[b * CAP + j : b * CAP + j + 1, :]
                moved_out[:, at] = value.astype(BF16)

    @pl.when(jnp.logical_not(has_next))
    def _():
        moved_out[...] = jnp.zeros_like(moved_out)

    @pl.when(has_prev)
    def _():
        for q in range(QUARTERS):
            back_all(q).wait_send()


def on_device(n_row, n_sec, layer_input, cotangent, route_weight, chosen, hot_expert, store_in, store_out):
    _, tokens, width = layer_input.shape
    ff = store_out.shape[1]
    top = chosen.shape[2]
    slots = n_row * CAP
    half = width // HALVES
    part = half // BANDS
    quarter = width // QUARTERS
    band = quarter // BANDS
    hbm = pl.BlockSpec(memory_space=pl.ANY)
    vmem = pl.BlockSpec(memory_space=pltpu.VMEM)
    dma = pltpu.SemaphoreType.DMA
    moved, grad = pl.pallas_call(
        functools.partial(expert_kernel, n_row, n_sec),
        out_shape=(
            pltpu.VMEM((tokens, width), BF16),
            pltpu.VMEM((top, tokens), F32),
        ),
        in_specs=[pl.BlockSpec(memory_space=pltpu.SMEM)] + [hbm] * 6,
        out_specs=(vmem, vmem),
        scratch_shapes=[
            pltpu.VMEM((top, tokens), jnp.int32),
            pltpu.VMEM((top, tokens), F32),
            pltpu.VMEM((tokens, width), BF16),
            pltpu.VMEM((tokens, width), BF16),
            pltpu.VMEM((width, 2 * ff), BF16),
            pltpu.VMEM((ff, width), BF16),
            pltpu.VMEM((2 * HALVES, n_row, ROWS, part), BF16),
            pltpu.VMEM((slots, width), BF16),
            pltpu.VMEM((slots, width), BF16),
            pltpu.VMEM((QUARTERS, n_row, ROWS, band), BF16),
            pltpu.VMEM((QUARTERS, n_row, ROWS, band), BF16),
            pltpu.VMEM((8, tokens), F32),
            pltpu.VMEM((8, tokens), F32),
            pltpu.VMEM((8, 128), F32),
            pltpu.VMEM((n_row, 8, 128), F32),
            dma((2, QUARTERS)),
            dma,
            dma((2,)),
            dma((2 * HALVES,)),
            dma((2 * HALVES,)),
            dma((2 * HALVES,)),
            dma((QUARTERS,)),
            dma((QUARTERS,)),
            dma,
            dma,
            dma,
            dma,
            dma,
            dma,
        ],
        compiler_params=pltpu.CompilerParams(
            collective_id=0, has_side_effects=True, vmem_limit_bytes=60 * 2**20
        ),
        cost_estimate=pl.CostEstimate(
            flops=10 * slots * width * ff, bytes_accessed=6 * width * ff, transcendentals=slots * ff
        ),
        name="expert",
    )(
        hot_expert,
        jnp.transpose(chosen[0]),
        jnp.transpose(route_weight[0]),
        layer_input[0],
        cotangent[0],
        store_in[0],
        store_out[0],
    )
    return (moved[None], jnp.transpose(grad)[None])


def token_select(block_c, hot, slot_count):
    count_tok, top_count = block_c.shape
    hit = (block_c == hot).astype(jnp.int32).reshape(-1)
    order = jnp.cumsum(hit) - hit
    held = hit * (order < slot_count).astype(jnp.int32)
    slots = (order[None, :] == jnp.arange(slot_count, dtype=jnp.int32)[:, None]).astype(
        jnp.int32
    ) * held[None, :]
    tsel = jnp.sum(slots.reshape(slot_count, count_tok, top_count), axis=2)
    return (tsel, held.reshape(count_tok, top_count))


def on_device_narrow(layer_input, cotangent, route_weight, chosen, hot_expert, store_in, store_out):
    tokens_here = layer_input[0]
    cot_here = cotangent[0]
    width = tokens_here.shape[1]
    num_row = lax.axis_size("row")
    size = lax.axis_size("section")
    tsel, held = token_select(chosen[0], hot_expert[0], CAP)
    pick = tsel.astype(BF16)
    rows = jnp.concatenate(
        [jnp.dot(pick, part, preferred_element_type=F32).astype(BF16) for part in (tokens_here, cot_here)], axis=1
    )
    both = lax.all_gather(rows, "row", axis=0, tiled=True)
    all_x, all_g = both[:, :width], both[:, width:]
    w_gate, w_up, w_out = store_in[0, 0], store_in[0, 1], store_out[0]
    gate = jnp.dot(all_x, w_gate, preferred_element_type=F32)
    upper = jnp.dot(all_x, w_up, preferred_element_type=F32)
    sig = jax.nn.sigmoid(gate)
    hidden = (gate * sig * upper).astype(BF16)
    d_hidden = lax.dot_general(all_g, w_out, LAST, preferred_element_type=F32)
    d_gate = (d_hidden * upper * sig * (1.0 + gate * (1.0 - sig))).astype(BF16)
    d_up = (d_hidden * gate * sig).astype(BF16)
    back_part = lax.dot_general(d_gate, w_gate, LAST, preferred_element_type=F32) + lax.dot_general(
        d_up, w_up, LAST, preferred_element_type=F32
    )
    score_part = jnp.sum(hidden.astype(F32) * d_hidden, axis=1)
    got_back = lax.all_to_all(
        back_part.reshape(num_row, CAP, width), "row", split_axis=0, concat_axis=0, tiled=True
    )
    got_score = lax.all_to_all(
        score_part.reshape(num_row, CAP), "row", split_axis=0, concat_axis=0, tiled=True
    )
    back_rows = jnp.sum(got_back, axis=0).astype(BF16)
    slot_score = jnp.sum(got_score, axis=0)
    back_tok = jnp.dot(pick.T, back_rows, preferred_element_type=F32)
    score_tok = jnp.sum(tsel.astype(F32).T * slot_score[None, :], axis=1)
    weight_tok = jnp.sum(held.astype(F32) * route_weight[0], axis=1)
    moved = (cot_here.astype(F32) + weight_tok[:, None] * back_tok).astype(BF16)
    route_grad = held.astype(F32) * score_tok[:, None]
    back_cot = lax.ppermute(moved, "section", [(i, i - 1) for i in range(1, size)])
    return (back_cot[None], route_grad[None])


def solution(mesh):
    n_row, n_sec = mesh.shape["row"], mesh.shape["section"]

    def body(layer_input, cotangent, route_weight, chosen, hot_expert, store_in, store_out):
        args = (layer_input, cotangent, route_weight, chosen, hot_expert, store_in, store_out)
        if store_out.shape[1] % 128 or n_row * CAP > 128:
            return on_device_narrow(*args)
        return on_device(n_row, n_sec, *args)

    in_specs = (
        P("section", "row", None),
        P("section", "row", None),
        P("section", "row", None),
        P("section", "row", None),
        P("section"),
        P("section", None, None, "row"),
        P("section", "row", None),
    )
    out_specs = (P("section", "row", None), P("section", "row", None))
    return jax.shard_map(body, mesh=mesh, in_specs=in_specs, out_specs=out_specs, check_vma=False)
```

```python
import functools

import jax
import jax.numpy as jnp
from jax import lax
from jax.experimental import pallas as pl
from jax.experimental.pallas import tpu as pltpu
from jax.sharding import PartitionSpec as P

CAP = 2
MESH = pl.DeviceIdType.MESH
F32 = jnp.float32
BF16 = jnp.bfloat16
ROWS = 16
BANDS = ROWS // CAP
QUARTERS = 4
HALVES = 2
LAST = (((1,), (1,)), ((), ()))


def iota(shape, dim):
    return lax.broadcasted_iota(jnp.int32, shape, dim)


def expert_kernel(
    n_row, n_sec, hot_ref, chosen_hbm, weight_hbm, x_hbm, cot_hbm, win_hbm, wout_hbm,
    moved_out, grad_out,
    chosen_ref, weight_ref, x_v, cot_v, win_v, wout_v, gath, xs, gs, pack, land,
    scale_v, scale_land, score_v, score_land,
    win_sem, wout_sem, pick_sem, t_sem, gath_send, gath_recv, back_send, back_recv, score_send, score_recv,
    small_send, small_recv, shift_send, shift_recv,
):
    sec = lax.axis_index("section")
    me = lax.axis_index("row")
    tokens, width = x_v.shape
    slots = n_row * CAP
    half = width // HALVES
    part = half // BANDS
    quarter = width // QUARTERS
    band = quarter // BANDS

    def win_copy(i, c):
        rows = pl.ds(c * quarter, quarter)
        return pltpu.make_async_copy(win_hbm.at[i, rows], win_v.at[i, rows], win_sem.at[i, c])

    wout_copy = pltpu.make_async_copy(wout_hbm, wout_v, wout_sem)
    def token_copy(k):
        source, to = ((x_hbm, x_v), (cot_hbm, cot_v))[k // HALVES]
        cols = pl.ds(k % HALVES * half, half)
        return pltpu.make_async_copy(source.at[:, cols], to.at[:, cols], t_sem.at[k])

    pick_copies = [
        pltpu.make_async_copy(source, to, pick_sem.at[i])
        for i, (source, to) in enumerate(((chosen_hbm, chosen_ref), (weight_hbm, weight_ref)))
    ]
    for copy in pick_copies:
        copy.start()
    for k in range(2 * HALVES):
        token_copy(k).start()

    has_prev = sec > 0
    has_next = sec < n_sec - 1
    barrier = pltpu.get_barrier_semaphore()

    @pl.loop(1, n_row)
    def _(i):
        pl.semaphore_signal(
            barrier, inc=1, device_id={"section": sec, "row": lax.rem(me + i, n_row)}, device_id_type=MESH
        )

    @pl.when(has_prev)
    def _():
        @pl.loop(0, n_row)
        def _(r):
            pl.semaphore_signal(barrier, inc=1, device_id={"section": sec - 1, "row": r}, device_id_type=MESH)

    @pl.when(has_next)
    def _():
        @pl.loop(0, n_row)
        def _(r):
            pl.semaphore_signal(barrier, inc=1, device_id={"section": sec + 1, "row": r}, device_id_type=MESH)

    for copy in pick_copies:
        copy.wait()

    hit = (chosen_ref[...] == hot_ref[0]).astype(F32)
    hit_tok = jnp.sum(hit, axis=0, keepdims=True)
    before = (iota((tokens, tokens), 0) < iota((tokens, tokens), 1)).astype(BF16)
    order = jnp.dot(
        jnp.broadcast_to(hit_tok, (ROWS, tokens)).astype(BF16), before, preferred_element_type=F32
    )[0:1]
    picks = [jnp.where(order == float(j), hit_tok, 0.0) for j in range(CAP)]
    held = hit * sum(picks)
    weight_tok = jnp.sum(held * weight_ref[...], axis=0, keepdims=True)
    row8 = iota((8, tokens), 0)
    scale = jnp.zeros((8, tokens), F32)
    for j in range(CAP):
        scale = scale + jnp.where(row8 == j, weight_tok * picks[j], 0.0)
    scale_v[...] = scale

    lead = iota((ROWS, tokens), 0)
    ones = []
    for c in range(BANDS):
        one = jnp.zeros((ROWS, tokens), F32)
        for j in range(CAP):
            one = one + jnp.where(lead == c * CAP + j, picks[j], 0.0)
        ones.append(one.astype(BF16))

    def held_rows(k):
        source = (x_v, cot_v)[k // HALVES]
        block = jnp.zeros((ROWS, part), F32)
        for c in range(BANDS):
            at = k % HALVES * half + c * part
            block = block + jnp.dot(ones[c], source[:, at : at + part], preferred_element_type=F32)
        gath[k, 0] = block.astype(BF16)

    def send_rows(k):
        @pl.loop(1, n_row)
        def _(i):
            gath_copy(k, i).start()

    def gath_copy(k, i):
        return pltpu.make_async_remote_copy(
            gath.at[k, 0], gath.at[k, i], gath_send.at[k], gath_recv.at[k],
            device_id={"section": sec, "row": lax.rem(me + n_row - i, n_row)}, device_id_type=MESH,
        )

    def gath_all(k):
        others = gath.at[k, pl.ds(1, n_row - 1)]
        return pltpu.make_async_remote_copy(
            others, others, gath_send.at[k], gath_recv.at[k],
            device_id={"section": sec, "row": me}, device_id_type=MESH,
        )

    prev = {"section": sec - 1, "row": me}
    shift = pltpu.make_async_remote_copy(
        cot_hbm, moved_out, shift_send, shift_recv, device_id=prev, device_id_type=MESH
    )
    small = pltpu.make_async_remote_copy(
        scale_v, scale_land, small_send, small_recv, device_id=prev, device_id_type=MESH
    )

    for k in range(2 * HALVES):
        token_copy(k).wait()
        if k < HALVES:
            held_rows(k)
    for c in range(QUARTERS):
        win_copy(0, c).start()
        win_copy(1, c).start()
    wout_copy.start()

    sides = has_prev.astype(jnp.int32) + has_next.astype(jnp.int32)
    pl.semaphore_wait(barrier, n_row - 1 + n_row * sides)
    for k in range(HALVES):
        send_rows(k)

    for k in range(HALVES, 2 * HALVES):
        held_rows(k)
        send_rows(k)

    @pl.when(has_prev)
    def _():
        shift.start()
        small.start()

    to_row = iota((BANDS * slots, n_row * ROWS), 0)
    slot = lax.rem(to_row, slots)
    away = lax.rem(slot // CAP - me + n_row, n_row)
    want = away * ROWS + (to_row // slots) * CAP + lax.rem(slot, CAP)
    spread = (iota((BANDS * slots, n_row * ROWS), 1) == want).astype(BF16)

    def gathered(k, rows_ref, h):
        gath_all(k).wait_recv()
        everyone = gath[k].reshape(n_row * ROWS, part)
        rows = jnp.dot(spread, everyone, preferred_element_type=F32).astype(BF16)
        for c in range(BANDS):
            at = h * half + c * part
            rows_ref[:, at : at + part] = rows[c * slots : (c + 1) * slots]

    gate = up = None
    for c in range(QUARTERS):
        cols = slice(c * quarter, (c + 1) * quarter)
        if c % (QUARTERS // HALVES) == 0:
            gathered(c // (QUARTERS // HALVES), xs, c // (QUARTERS // HALVES))
        win_copy(0, c).wait()
        win_copy(1, c).wait()
        g_part = jnp.dot(xs[:, cols], win_v[0, cols, :], preferred_element_type=F32)
        u_part = jnp.dot(xs[:, cols], win_v[1, cols, :], preferred_element_type=F32)
        gate = g_part if gate is None else gate + g_part
        up = u_part if up is None else up + u_part

    gathered(2, gs, 0)
    gathered(3, gs, 1)
    wout_copy.wait()
    dh = lax.dot_general(wout_v[...], gs[...], LAST, preferred_element_type=F32).T

    sig = jax.nn.sigmoid(gate)
    hidden = (gate * sig * up).astype(BF16)
    dgate = (dh * up * sig * (1.0 + gate * (1.0 - sig))).astype(BF16)
    dup = (dh * gate * sig).astype(BF16)
    score = jnp.sum(hidden.astype(F32) * dh, axis=1, keepdims=True)
    diag = iota((slots, 128), 0) == iota((slots, 128), 1)
    score_row = jnp.sum(jnp.where(diag, score, 0.0), axis=0, keepdims=True)
    score_v[...] = jnp.broadcast_to(score_row, score_v.shape)

    score_land[0] = score_v[...]

    def score_copy(i):
        return pltpu.make_async_remote_copy(
            score_v, score_land.at[i], score_send, score_recv,
            device_id={"section": sec, "row": lax.rem(me + n_row - i, n_row)}, device_id_type=MESH,
        )

    def score_all():
        others = score_land.at[pl.ds(1, n_row - 1)]
        return pltpu.make_async_remote_copy(
            others, others, score_send, score_recv,
            device_id={"section": sec, "row": me}, device_id_type=MESH,
        )

    @pl.loop(1, n_row)
    def _(i):
        score_copy(i).start()

    def back_copy(q, r):
        return pltpu.make_async_remote_copy(
            pack.at[q, r], land.at[q, me], back_send.at[q], back_recv.at[q],
            device_id={"section": sec - 1, "row": r}, device_id_type=MESH,
        )

    def back_all(q):
        return pltpu.make_async_remote_copy(
            pack.at[q], land.at[q], back_send.at[q], back_recv.at[q],
            device_id={"section": sec - 1, "row": me}, device_id_type=MESH,
        )

    @pl.when(has_prev)
    def _():
        out_row = iota((n_row * ROWS, BANDS * slots), 0)
        inner = lax.rem(out_row, ROWS)
        source = (inner // CAP) * slots + (out_row // ROWS) * CAP + lax.rem(inner, CAP)
        perm = (iota((n_row * ROWS, BANDS * slots), 1) == source).astype(BF16)
        for q in range(QUARTERS):
            rows = slice(q * quarter, (q + 1) * quarter)
            total = lax.dot_general(win_v[0, rows, :], dgate, LAST, preferred_element_type=F32)
            total = total + lax.dot_general(win_v[1, rows, :], dup, LAST, preferred_element_type=F32)
            back = total.T.astype(BF16)
            stack = jnp.concatenate([back[:, b * band : (b + 1) * band] for b in range(BANDS)], axis=0)
            packed = jnp.dot(perm, stack, preferred_element_type=F32).astype(BF16)
            pack[q] = packed.reshape(n_row, ROWS, band)

            @pl.loop(0, n_row)
            def _(i):
                back_copy(q, lax.rem(me + i, n_row)).start()

    score_all().wait_recv()
    sums = jnp.sum(score_land[...], axis=0)
    lane = iota(sums.shape, 1)
    grad_tok = jnp.zeros((1, tokens), F32)
    for j in range(CAP):
        mine = jnp.sum(jnp.where(lane == me * CAP + j, sums, 0.0), axis=1, keepdims=True)[0:1]
        grad_tok = grad_tok + picks[j] * mine
    grad_out[...] = held * grad_tok

    for k in range(2 * HALVES):
        gath_all(k).wait_send()
    score_all().wait_send()

    @pl.when(has_prev)
    def _():
        small.wait_send()
        shift.wait_send()

    @pl.when(has_next)
    def _():
        small.wait_recv()
        diag = iota((tokens, tokens), 0) == iota((tokens, tokens), 1)
        scales = []
        for j in range(CAP):
            col = jnp.sum(jnp.where(diag, scale_land[j : j + 1, :], 0.0), axis=1, keepdims=True)
            scales.append(jnp.broadcast_to(col, (tokens, band)))
        shift.wait_recv()
        for q in range(QUARTERS):
            back_all(q).wait_recv()
            rows = jnp.sum(land[q].astype(F32), axis=0).astype(BF16).astype(F32)
            for b in range(BANDS):
                at = slice(q * quarter + b * band, q * quarter + (b + 1) * band)
                value = moved_out[:, at].astype(F32)
                for j in range(CAP):
                    value = value + scales[j] * rows[b * CAP + j : b * CAP + j + 1, :]
                moved_out[:, at] = value.astype(BF16)

    @pl.when(jnp.logical_not(has_next))
    def _():
        moved_out[...] = jnp.zeros_like(moved_out)

    @pl.when(has_prev)
    def _():
        for q in range(QUARTERS):
            back_all(q).wait_send()


def on_device(n_row, n_sec, layer_input, cotangent, route_weight, chosen, hot_expert, store_in, store_out):
    _, tokens, width = layer_input.shape
    ff = store_out.shape[1]
    top = chosen.shape[2]
    slots = n_row * CAP
    half = width // HALVES
    part = half // BANDS
    quarter = width // QUARTERS
    band = quarter // BANDS
    hbm = pl.BlockSpec(memory_space=pl.ANY)
    vmem = pl.BlockSpec(memory_space=pltpu.VMEM)
    dma = pltpu.SemaphoreType.DMA
    moved, grad = pl.pallas_call(
        functools.partial(expert_kernel, n_row, n_sec),
        out_shape=(
            pltpu.VMEM((tokens, width), BF16),
            pltpu.VMEM((top, tokens), F32),
        ),
        in_specs=[pl.BlockSpec(memory_space=pltpu.SMEM)] + [hbm] * 6,
        out_specs=(vmem, vmem),
        scratch_shapes=[
            pltpu.VMEM((top, tokens), jnp.int32),
            pltpu.VMEM((top, tokens), F32),
            pltpu.VMEM((tokens, width), BF16),
            pltpu.VMEM((tokens, width), BF16),
            pltpu.VMEM((2, width, ff), BF16),
            pltpu.VMEM((ff, width), BF16),
            pltpu.VMEM((2 * HALVES, n_row, ROWS, part), BF16),
            pltpu.VMEM((slots, width), BF16),
            pltpu.VMEM((slots, width), BF16),
            pltpu.VMEM((QUARTERS, n_row, ROWS, band), BF16),
            pltpu.VMEM((QUARTERS, n_row, ROWS, band), BF16),
            pltpu.VMEM((8, tokens), F32),
            pltpu.VMEM((8, tokens), F32),
            pltpu.VMEM((8, 128), F32),
            pltpu.VMEM((n_row, 8, 128), F32),
            dma((2, QUARTERS)),
            dma,
            dma((2,)),
            dma((2 * HALVES,)),
            dma((2 * HALVES,)),
            dma((2 * HALVES,)),
            dma((QUARTERS,)),
            dma((QUARTERS,)),
            dma,
            dma,
            dma,
            dma,
            dma,
            dma,
        ],
        compiler_params=pltpu.CompilerParams(
            collective_id=0, has_side_effects=True, vmem_limit_bytes=60 * 2**20
        ),
        cost_estimate=pl.CostEstimate(
            flops=10 * slots * width * ff, bytes_accessed=6 * width * ff, transcendentals=slots * ff
        ),
        name="expert",
    )(
        hot_expert,
        jnp.transpose(chosen[0]),
        jnp.transpose(route_weight[0]),
        layer_input[0],
        cotangent[0],
        store_in[0],
        store_out[0],
    )
    return (moved[None], jnp.transpose(grad)[None])


def token_select(block_c, hot, slot_count):
    count_tok, top_count = block_c.shape
    hit = (block_c == hot).astype(jnp.int32).reshape(-1)
    order = jnp.cumsum(hit) - hit
    held = hit * (order < slot_count).astype(jnp.int32)
    slots = (order[None, :] == jnp.arange(slot_count, dtype=jnp.int32)[:, None]).astype(
        jnp.int32
    ) * held[None, :]
    tsel = jnp.sum(slots.reshape(slot_count, count_tok, top_count), axis=2)
    return (tsel, held.reshape(count_tok, top_count))


def on_device_narrow(layer_input, cotangent, route_weight, chosen, hot_expert, store_in, store_out):
    tokens_here = layer_input[0]
    cot_here = cotangent[0]
    width = tokens_here.shape[1]
    num_row = lax.axis_size("row")
    size = lax.axis_size("section")
    tsel, held = token_select(chosen[0], hot_expert[0], CAP)
    pick = tsel.astype(BF16)
    rows = jnp.concatenate(
        [jnp.dot(pick, part, preferred_element_type=F32).astype(BF16) for part in (tokens_here, cot_here)], axis=1
    )
    both = lax.all_gather(rows, "row", axis=0, tiled=True)
    all_x, all_g = both[:, :width], both[:, width:]
    w_gate, w_up, w_out = store_in[0, 0], store_in[0, 1], store_out[0]
    gate = jnp.dot(all_x, w_gate, preferred_element_type=F32)
    upper = jnp.dot(all_x, w_up, preferred_element_type=F32)
    sig = jax.nn.sigmoid(gate)
    hidden = (gate * sig * upper).astype(BF16)
    d_hidden = lax.dot_general(all_g, w_out, LAST, preferred_element_type=F32)
    d_gate = (d_hidden * upper * sig * (1.0 + gate * (1.0 - sig))).astype(BF16)
    d_up = (d_hidden * gate * sig).astype(BF16)
    back_part = lax.dot_general(d_gate, w_gate, LAST, preferred_element_type=F32) + lax.dot_general(
        d_up, w_up, LAST, preferred_element_type=F32
    )
    score_part = jnp.sum(hidden.astype(F32) * d_hidden, axis=1)
    got_back = lax.all_to_all(
        back_part.reshape(num_row, CAP, width), "row", split_axis=0, concat_axis=0, tiled=True
    )
    got_score = lax.all_to_all(
        score_part.reshape(num_row, CAP), "row", split_axis=0, concat_axis=0, tiled=True
    )
    back_rows = jnp.sum(got_back, axis=0).astype(BF16)
    slot_score = jnp.sum(got_score, axis=0)
    back_tok = jnp.dot(pick.T, back_rows, preferred_element_type=F32)
    score_tok = jnp.sum(tsel.astype(F32).T * slot_score[None, :], axis=1)
    weight_tok = jnp.sum(held.astype(F32) * route_weight[0], axis=1)
    moved = (cot_here.astype(F32) + weight_tok[:, None] * back_tok).astype(BF16)
    route_grad = held.astype(F32) * score_tok[:, None]
    back_cot = lax.ppermute(moved, "section", [(i, i - 1) for i in range(1, size)])
    return (back_cot[None], route_grad[None])


def solution(mesh):
    n_row, n_sec = mesh.shape["row"], mesh.shape["section"]

    def body(layer_input, cotangent, route_weight, chosen, hot_expert, store_in, store_out):
        args = (layer_input, cotangent, route_weight, chosen, hot_expert, store_in, store_out)
        if store_out.shape[1] % 128 or n_row * CAP > 128:
            return on_device_narrow(*args)
        return on_device(n_row, n_sec, *args)

    in_specs = (
        P("section", "row", None),
        P("section", "row", None),
        P("section", "row", None),
        P("section", "row", None),
        P("section"),
        P("section", None, None, "row"),
        P("section", "row", None),
    )
    out_specs = (P("section", "row", None), P("section", "row", None))
    return jax.shard_map(body, mesh=mesh, in_specs=in_specs, out_specs=out_specs, check_vma=False)
```
